256 devices in a mesh: ctx: 32 (over z_lo, x, y), exp: 8 (over z_hi, core).
Axes of the slice: x: 4, y: 4, z: 8 (z_hi: 4, z_lo: 2; z = z_hi * 2 + z_lo), core: 2. Of those that a mesh axis runs over, the one named last changes fastest.
Arguments:
- query: bfloat16 [4096, 2048], P('ctx', 'exp'), may hold values from -5 to 5
- keys: bfloat16 [4096, 2048], P('ctx', 'exp'), may hold values from -5 to 5
- values: bfloat16 [4096, 2048], P('ctx', 'exp'), may hold values from -5 to 5
- resid: bfloat16 [4096, 4096], P('ctx'), may hold values from -6 to 6
- flags: int32 [4096], P('ctx'), may hold values from 0 to 1, as said below
- routes: int32 [4096, 6], P('ctx'), may hold values from 0 to 63, all different within a row; in each aligned block of 16 rows (0 to 15, 16 to 31, ...) at most 2 rows name the same one
- gates: bfloat16 [4096, 6], P('ctx'), may hold values from 0.049804688 to 0.3984375
- out_weight: bfloat16 [2048, 4096], P('exp'), may hold values from -0.125 to 0.125
- norm_gain: float32 [4096], replicated, may hold values from 0.1 to 1.9
- img_gate: bfloat16 [4096, 5504], P('exp', 'ctx'), may hold values from -0.09375 to 0.09375
- img_up: bfloat16 [4096, 5504], P('exp', 'ctx'), may hold values from -0.09375 to 0.09375
- img_down: bfloat16 [4096, 5504], P('exp', 'ctx'), may hold values from -0.078125 to 0.078125
- exp_gate: bfloat16 [256, 4096, 352], P(('ctx', 'exp')), may hold values from -0.09375 to 0.09375
- exp_up: bfloat16 [256, 4096, 352], P(('ctx', 'exp')), may hold values from -0.09375 to 0.09375
- exp_down: bfloat16 [256, 352, 4096], P(('ctx', 'exp')), may hold values from -0.15625 to 0.15625
Outputs:
- layer_out: bfloat16 [4096, 4096], P(('ctx', 'exp'))
The draws below stay inside these ranges and needn't reach their ends.
Inputs may be any that keep to these rules, and one draw needn't show every extreme that they name: `routes`: in each aligned block of 16 rows, no expert is named by more than 2 rows. `flags`: in each aligned block of 16 positions at most 8 are image positions; some block holds exactly 8.
All inputs are finite; a program needn't handle non-finite values.
Results may differ from the reference program's by a relative error of at most 0.02.
Values may be sent and summed in bfloat16 or wider, within the bound.
A program may use at most 128 MiB of HBM per device.

```python
import math
import jax
import jax.numpy as jnp
import numpy as np
from jax import lax

D = 4096
HEADS = 16
HEAD_DIM = 128
IMG_HIDDEN = 5504
EXP_HIDDEN = 1408
EXPERTS = 64
TOP = 6
ROWS = 16
SEQ = 4096
CAP = 2
IMG_CAP = 8
IMG_BLOCK = 172
SPLIT = 4
EXP_PIECE = 352
N_CTX = 32


def draw_query(key, part):
    key = jax.random.fold_in(key, 7)
    result = jnp.clip(jax.random.normal(key, (SEQ, HEADS * HEAD_DIM), jnp.float32), -4.0, 4.0)
    return result.astype(jnp.bfloat16)


def draw_keys(key, part):
    key = jax.random.fold_in(key, 13)
    result = jnp.clip(jax.random.normal(key, (SEQ, HEADS * HEAD_DIM), jnp.float32), -4.0, 4.0)
    return result.astype(jnp.bfloat16)


def draw_flags(key, part):
    key = jax.random.fold_in(key, 21)
    blocks = SEQ // ROWS
    order_key, count_key, forced_key = jax.random.split(key, 3)
    noise = jax.random.randint(order_key, (blocks, ROWS), 0, 1 << 20)
    scores = noise * ROWS + jnp.arange(ROWS, dtype=jnp.int32)[None, :]
    order = jnp.argsort(scores, axis=1, stable=True)
    place = jnp.argsort(order, axis=1, stable=True)
    counts = jax.random.randint(count_key, (blocks,), 0, IMG_CAP + 1)
    forced = jax.random.randint(forced_key, (), 0, blocks)
    counts = jnp.where(jnp.arange(blocks, dtype=jnp.int32) == forced, IMG_CAP, counts)
    return (place < counts[:, None]).astype(jnp.int32).reshape(SEQ)


def levels(stream_key, shape, pieces, least, largest):
    loudness = 1.0
    for axis_at, shards_of in pieces:
        steps = jax.random.uniform(jax.random.fold_in(jax.random.fold_in(stream_key, 6), axis_at), (shards_of,), jnp.float32, least / len(pieces), largest / len(pieces))
        loudness = loudness * jnp.repeat(jnp.exp(steps), shape[axis_at] // shards_of).reshape((-1,) + (1,) * (len(shape) - 1 - axis_at))
    return loudness


def routed_block(own_key, own, number, rows, count, top, limit, skew):
    order = jax.random.permutation(own_key, count)
    heavy_load, common = shares(count, rows * top, limit, skew, True), shares(count, rows * top, limit, skew, False)
    places = jnp.arange(count)

    def named(sizes, offset_by):
        used = int((sizes > 0).sum())
        fixed = max(1, used // 4)
        shifted = fixed + (places - fixed + offset_by * (used - fixed)) % max(1, count - fixed)
        return jnp.zeros((count,), jnp.int32).at[order[jnp.where(places < fixed, places, shifted)]].set(jnp.asarray(sizes, jnp.int32))

    sizes = jnp.where(number % 4 == 0, named(heavy_load, number // 4), named(common, number - number // 4 - 1))
    mixed = jax.random.permutation(jax.random.fold_in(own, 3), count)
    donor, receiver = mixed[0:count // 2 * 2:2], mixed[1:count // 2 * 2:2]
    slack = jnp.minimum(sizes[donor] - 1, limit - sizes[receiver]) // 2
    slack = jnp.where((donor == order[0]) | (receiver == order[0]) | (sizes[receiver] == 0), 0, jnp.maximum(slack, 0))
    shifted = jax.random.randint(jax.random.fold_in(own, 4), (count // 2,), 0, 1 << 20) % (slack + 1)
    sizes = sizes.at[donor].add(-shifted).at[receiver].add(shifted)
    items = jnp.searchsorted(jnp.cumsum(sizes), jnp.arange(rows * top), side="right").astype(jnp.int32)
    listing = items.reshape(top, rows).T
    listing = listing[jax.random.permutation(jax.random.fold_in(own, 1), rows)]
    offset_by = jax.random.randint(jax.random.fold_in(own, 2), (rows, 1), 0, top)
    return jnp.take_along_axis(listing, (jnp.arange(top)[None, :] + offset_by) % top, axis=1)


def shares(count, total, most, skew, full):
    weights = [(1 << 20) // math.isqrt(standing ** skew) + 1 for standing in range(1, count + 1)]
    largest = most if full else min(most, max(-(-total // count), total * weights[0] // sum(weights)))
    least = 1 if total - largest >= count - 1 else 0
    holding, rest = [largest] + [least] * (count - 1), total - largest - least * (count - 1)
    while rest > 0:
        movable = [i for i in range(1, count) if holding[i] < largest] or [i for i in range(1, count) if holding[i] < most]
        pool, left = sum([weights[i] for i in movable]), rest
        for i in movable:
            more = min(most - holding[i], max(1, left * weights[i] // pool), rest)
            holding[i] = holding[i] + more
            rest = rest - more
    return np.array(holding)


def scatter_about(stream_key, dims, scale, limit, cuts=(), held_as=jnp.bfloat16):
    values = scale * jax.random.normal(stream_key, dims, jnp.float32)
    if cuts:
        values = values * levels(stream_key, dims, cuts, -0.22, 0.18)
    return jnp.clip(values, -limit, limit).astype(held_as)


def setup_inputs(seed: int = 0) -> dict:
    arg_keys = jax.random.split(jax.random.key(seed), 16)
    query = draw_query(jax.random.fold_in(arg_keys[15], 71), 0)
    keys = draw_keys(jax.random.fold_in(arg_keys[15], 71), 0)
    values = scatter_about(arg_keys[2], (SEQ, HEADS * HEAD_DIM), 1.0, 5.0, ((0, 32), (1, 8)))
    resid = scatter_about(arg_keys[3], (SEQ, D), 1.0, 6.0, ((0, 32),))
    flags = draw_flags(jax.random.fold_in(arg_keys[15], 71), 0)
    routes_keys = jax.random.split(jax.random.fold_in(arg_keys[5], 1), SEQ // ROWS)
    routes_turns = jax.random.permutation(jax.random.fold_in(arg_keys[5], 3), SEQ // ROWS)
    routes = jax.vmap(lambda own, number: routed_block(jax.random.fold_in(arg_keys[5], 2), own, number, ROWS, EXPERTS, TOP, CAP, 2))(routes_keys, routes_turns).reshape((SEQ, TOP))
    gates = jnp.clip(0.049804688 + 0.3486328 * jax.random.uniform(arg_keys[6], (SEQ, TOP), jnp.float32) ** levels(arg_keys[6], (SEQ, TOP), ((0, 32),), -0.2, 0.2), 0.049804688, 0.3984375).astype(jnp.bfloat16)
    out_weight = scatter_about(arg_keys[7], (HEADS * HEAD_DIM, D), (HEADS * HEAD_DIM) ** -0.5, 0.125, ((0, 8),))
    norm_gain = jnp.clip(1.0 + 0.18 * jax.random.normal(arg_keys[8], (D,), jnp.float32), 0.1, 1.9)
    img_gate = scatter_about(arg_keys[9], (D, IMG_HIDDEN), D ** -0.5, 0.09375, ((0, 8), (1, 32)))
    img_up = scatter_about(arg_keys[10], (D, IMG_HIDDEN), D ** -0.5, 0.09375, ((0, 8), (1, 32)))
    img_down = scatter_about(arg_keys[11], (D, IMG_HIDDEN), IMG_HIDDEN ** -0.5, 0.078125, ((0, 8), (1, 32)))
    exp_gate = scatter_about(arg_keys[12], (EXPERTS * SPLIT, D, EXP_PIECE), D ** -0.5, 0.09375, ((0, 256),))
    exp_up = scatter_about(arg_keys[13], (EXPERTS * SPLIT, D, EXP_PIECE), D ** -0.5, 0.09375, ((0, 256),))
    exp_down = scatter_about(arg_keys[14], (EXPERTS * SPLIT, EXP_PIECE, D), EXP_HIDDEN ** -0.5, 0.15625, ((0, 256),))
    return dict(query=query, keys=keys, values=values, resid=resid, flags=flags, routes=routes, gates=gates, out_weight=out_weight, norm_gain=norm_gain, img_gate=img_gate, img_up=img_up, img_down=img_down, exp_gate=exp_gate, exp_up=exp_up, exp_down=exp_down)


NEGATIVE = -1e+30
EPSILON = 1e-05

def attention(query, keys, values):
    score_scale = 1.0 / math.sqrt(HEAD_DIM)
    position = jnp.arange(SEQ, dtype=jnp.int32)
    allowed = position[None, :] <= position[:, None]
    query_heads = query.reshape(SEQ, HEADS, HEAD_DIM).transpose(1, 0, 2)
    key_heads = keys.reshape(SEQ, HEADS, HEAD_DIM).transpose(1, 0, 2)
    value_heads = values.reshape(SEQ, HEADS, HEAD_DIM).transpose(1, 0, 2)

    def one_head(bundle):
        query_head, key_head, value_head = bundle
        scores = jnp.dot(query_head, key_head.T, preferred_element_type=jnp.float32) * score_scale
        scores = jnp.where(allowed, scores, NEGATIVE)
        row_max = lax.optimization_barrier(jnp.max(scores, axis=-1, keepdims=True))
        weights = jnp.where(allowed, jnp.exp(scores - row_max), 0.0)
        denom = lax.optimization_barrier(jnp.sum(weights, axis=-1, keepdims=True))
        result = jnp.dot(weights.astype(jnp.bfloat16), value_head, preferred_element_type=jnp.float32)
        return result / denom
    heads_out = lax.map(one_head, (query_heads, key_heads, value_heads))
    return heads_out.transpose(1, 0, 2).reshape(SEQ, HEADS * HEAD_DIM).astype(jnp.bfloat16)

def reference(query, keys, values, resid, flags, routes, gates, out_weight, norm_gain, img_gate, img_up, img_down, exp_gate, exp_up, exp_down):
    attended = attention(query, keys, values)
    hidden_state = resid.astype(jnp.float32) + jnp.dot(attended, out_weight, preferred_element_type=jnp.float32)
    power = lax.optimization_barrier(jnp.mean(hidden_state * hidden_state, axis=-1, keepdims=True))
    normed = (hidden_state * lax.rsqrt(power + EPSILON) * norm_gain).astype(jnp.bfloat16)
    image_act = (jax.nn.silu(jnp.dot(normed, img_gate, preferred_element_type=jnp.float32)) * jnp.dot(normed, img_up, preferred_element_type=jnp.float32)).astype(jnp.bfloat16)

    def add_block(carried, block_index):
        offset = block_index * IMG_BLOCK
        portion = lax.dynamic_slice_in_dim(image_act, offset, IMG_BLOCK, 1)
        weight_block = lax.dynamic_slice_in_dim(img_down, offset, IMG_BLOCK, 1)
        partial_value = lax.dot_general(portion, weight_block, (((1,), (1,)), ((), ())), preferred_element_type=jnp.float32)
        rounded = lax.optimization_barrier(partial_value.astype(jnp.bfloat16))
        return (carried + rounded.astype(jnp.float32), None)
    image_out, _ = lax.scan(add_block, jnp.zeros((SEQ, D), jnp.float32), jnp.arange(N_CTX, dtype=jnp.int32))
    blocks = SEQ // ROWS
    expert_ids = routes.reshape(blocks, ROWS * TOP)
    usable = jnp.broadcast_to((flags == 0).reshape(blocks, ROWS, 1), (blocks, ROWS, TOP)).reshape(blocks, ROWS * TOP)
    onehot = (expert_ids[:, :, None] == jnp.arange(EXPERTS, dtype=jnp.int32)[None, None, :]) & usable[:, :, None]
    counts = jnp.cumsum(onehot.astype(jnp.int32), axis=1)
    slot_rank = lax.optimization_barrier(jnp.sum(jnp.where(onehot, counts, 0), axis=2)) - 1
    block_index = jnp.arange(blocks, dtype=jnp.int32)[:, None]
    row_index = block_index * ROWS + jnp.arange(ROWS * TOP, dtype=jnp.int32)[None, :] // TOP
    slot_total = EXPERTS * blocks * CAP
    slot_id = jnp.where(usable, (expert_ids * blocks + block_index) * CAP + slot_rank, slot_total)
    slot_row = jnp.zeros((slot_total + 1,), jnp.int32).at[slot_id.reshape(-1)].set(row_index.reshape(-1))
    slot_gate = jnp.zeros((slot_total + 1,), jnp.float32).at[slot_id.reshape(-1)].set(jnp.where(usable, gates.reshape(blocks, ROWS * TOP).astype(jnp.float32), 0.0).reshape(-1))
    per_expert = blocks * CAP
    slot_row = slot_row[:slot_total].reshape(EXPERTS, per_expert)
    slot_gate = slot_gate[:slot_total].reshape(EXPERTS, per_expert)
    gate_pieces = exp_gate.reshape(EXPERTS, SPLIT, D, EXP_PIECE)
    up_pieces = exp_up.reshape(EXPERTS, SPLIT, D, EXP_PIECE)
    down_pieces = exp_down.reshape(EXPERTS, SPLIT, EXP_PIECE, D)

    def one_expert(carried, bundle):
        row_ids, row_weights, gate_w, up_w, down_w = bundle
        chosen = normed[row_ids]
        result = jnp.zeros((per_expert, D), jnp.float32)
        for part_index in range(SPLIT):
            active = (jax.nn.silu(jnp.dot(chosen, gate_w[part_index], preferred_element_type=jnp.float32)) * jnp.dot(chosen, up_w[part_index], preferred_element_type=jnp.float32)).astype(jnp.bfloat16)
            partial_value = jnp.dot(active, down_w[part_index], preferred_element_type=jnp.float32)
            rounded = lax.optimization_barrier(partial_value.astype(jnp.bfloat16))
            result = result + rounded.astype(jnp.float32)
        return (carried.at[row_ids].add(row_weights[:, None] * result), None)
    text_out, _ = lax.scan(one_expert, jnp.zeros((SEQ, D), jnp.float32), (slot_row, slot_gate, gate_pieces, up_pieces, down_pieces))
    layer_out = hidden_state + jnp.where(flags[:, None] == 1, image_out, text_out)
    return layer_out.astype(jnp.bfloat16)
```

```python
import functools
import math

import jax
import jax.numpy as jnp
from jax import lax
from jax.experimental import pallas as pl
from jax.experimental.pallas import tpu as pltpu
from jax.sharding import PartitionSpec as P

MESH = pl.DeviceIdType.MESH
HEAD_DIM = 128
NEGATIVE = -1e30
EPSILON = 1e-05
WIDTH = 4096
CHUNK = 1024
CHUNKS = WIDTH // CHUNK


class Place:
    def __init__(self):
        c, e = lax.axis_index("ctx"), lax.axis_index("exp")
        self.c, self.e = c, e
        self.zl, self.x, self.y = lax.div(c, 16), lax.rem(lax.div(c, 4), 4), lax.rem(c, 4)
        self.zh, self.k = lax.div(e, 2), lax.rem(e, 2)
        self.z = self.zh * 2 + self.zl

    def dev(self, dx=0, dy=0, dzl=0, dzh=0, dk=0):
        x, y = lax.rem(self.x + dx + 4, 4), lax.rem(self.y + dy + 4, 4)
        zl, zh, k = lax.rem(self.zl + dzl, 2), lax.rem(self.zh + dzh + 4, 4), lax.rem(self.k + dk, 2)
        return (zl * 16 + x * 4 + y, zh * 2 + k)


def remote(src, dst, send, recv, device):
    return pltpu.make_async_remote_copy(
        src_ref=src, dst_ref=dst, send_sem=send, recv_sem=recv, device_id=device, device_id_type=MESH
    )


def attention_kernel(
    q_ref, k_ref, v_ref, resid_ref, gain_ref, ow_ref,
    state_ref, normed_ref,
    kbuf, vbuf, qbuf, obuf, stat, rbuf, rstat, ow, res, att, pbuf, sbuf, tbuf, zbuf,
    kv_send, kv_recv, q_send, q_recv, o_send, o_recv, s_send, s_recv, c_send, c_recv, z_send, z_recv, local_sem,
):
    at = Place()
    load_w = pltpu.make_async_copy(ow_ref, ow, local_sem.at[0])
    load_w.start()
    load_r = pltpu.make_async_copy(resid_ref.at[pl.ds(pl.multiple_of(at.e * 16, 16), 16)], res, local_sem.at[1])
    load_r.start()
    barrier = pltpu.get_barrier_semaphore()
    partners = [at.dev(dx=d) for d in (1, 2, 3)]
    partners += [at.dev(dzl=j // 4, dy=j % 4) for j in range(1, 8)]
    partners += [at.dev(dk=1)] + [at.dev(dzh=d) for d in (1, 2, 3)]
    for device in partners:
        pl.semaphore_signal(barrier, inc=1, device_id=device, device_id_type=MESH)
    kbuf[0] = k_ref[...]
    vbuf[0] = v_ref[...]
    qbuf[0] = q_ref[...]
    pl.semaphore_wait(barrier, len(partners))

    kv = []
    for d in (1, 2, 3):
        kv.append(remote(k_ref, kbuf.at[d], kv_send.at[0, d], kv_recv.at[0, d], at.dev(dx=d)))
        kv.append(remote(v_ref, vbuf.at[d], kv_send.at[1, d], kv_recv.at[1, d], at.dev(dx=d)))
    qs = [None] + [
        remote(q_ref, qbuf.at[j], q_send.at[j], q_recv.at[j], at.dev(dzl=j // 4, dy=j % 4)) for j in range(1, 8)
    ]
    for j in range(1, 8):
        qs[j].start()
    for copy in kv:
        copy.start()

    rows = lax.broadcasted_iota(jnp.int32, (512, 128), 0)
    lanes = lax.broadcasted_iota(jnp.int32, (512, 128), 1)
    from_x = lax.rem(at.x - lax.div(rows, 128) + 4, 4)
    key_spot = (at.zl * 16 + from_x * 4 + at.y) * 128 + lax.rem(rows, 128) - lanes
    for copy in kv:
        copy.wait_recv()

    def back(j):
        device = at.dev(dzl=lax.div(j, 4), dy=4 - lax.rem(j, 4))
        return (
            remote(obuf.at[j], rbuf.at[j], o_send.at[j], o_recv.at[j], device),
            remote(stat.at[j], rstat.at[j], s_send.at[j], s_recv.at[j], device),
        )

    def one_block(j, _):
        @pl.when(j > 0)
        def _():
            remote(q_ref, qbuf.at[j], q_send.at[j], q_recv.at[j], at.dev(dzl=lax.div(j, 4), dy=lax.rem(j, 4))).wait_recv()

        q_zl = lax.rem(at.zl + lax.div(j, 4), 2)
        q_y = lax.rem(at.y + 4 - lax.rem(j, 4), 4)
        limit = (q_zl * 16 + at.x * 4 + q_y) * 128
        allowed = key_spot <= limit
        stats = []
        for h in range(2):
            cols = slice(h * HEAD_DIM, (h + 1) * HEAD_DIM)
            kh = kbuf[:, :, cols].reshape(512, HEAD_DIM)
            vh = vbuf[:, :, cols].reshape(512, HEAD_DIM)
            qh = qbuf[j, :, cols]
            s = lax.dot_general(kh, qh, (((1,), (1,)), ((), ())), preferred_element_type=jnp.float32)
            s = jnp.where(allowed, s * (1.0 / math.sqrt(HEAD_DIM)), NEGATIVE)
            m = jnp.max(s, axis=0, keepdims=True)
            p = jnp.where(allowed, jnp.exp(s - m), 0.0)
            l = jnp.sum(p, axis=0, keepdims=True)
            o = lax.dot_general(vh, p.astype(jnp.bfloat16), (((0,), (0,)), ((), ())), preferred_element_type=jnp.float32)
            obuf[j, cols, :] = o.astype(jnp.bfloat16)
            stats += [m, l]
        stat[j] = jnp.concatenate(stats + stats, axis=0)

        @pl.when(j > 0)
        def _():
            for copy in back(j):
                copy.start()

        return 0

    lax.fori_loop(0, 8, one_block, 0)
    rbuf[0] = obuf[0]
    rstat[0] = stat[0]
    for j in range(1, 8):
        for copy in back(j):
            copy.wait_recv()
    for h in range(2):
        cols = slice(h * HEAD_DIM, (h + 1) * HEAD_DIM)
        top = rstat[0, 2 * h:2 * h + 1, :]
        for j in range(1, 8):
            top = jnp.maximum(top, rstat[j, 2 * h:2 * h + 1, :])
        total = jnp.zeros((HEAD_DIM, 128), jnp.float32)
        denom = jnp.zeros((1, 128), jnp.float32)
        for j in range(8):
            w = jnp.exp(rstat[j, 2 * h:2 * h + 1, :] - top)
            denom += w * rstat[j, 2 * h + 1:2 * h + 2, :]
            total += w * rbuf[j, cols, :].astype(jnp.float32)
        att[cols, :] = (total / denom).astype(jnp.bfloat16)

    load_w.wait()
    load_r.wait()
    swaps, sums = [], []
    for n in range(CHUNKS):
        cols = pl.ds(n * CHUNK, CHUNK)
        part = lax.dot_general(
            att[...], ow[:, cols], (((0,), (0,)), ((), ())), preferred_element_type=jnp.float32
        ).astype(jnp.bfloat16)
        for b in range(8):
            pbuf[b % 2, b // 2, :, cols] = part[16 * b:16 * b + 16]
        copy = remote(pbuf.at[1 - at.k, :, :, cols], sbuf.at[:, :, cols], c_send.at[n], c_recv.at[n], at.dev(dk=1))
        copy.start()
        swaps.append(copy)
    for n in range(CHUNKS):
        cols = pl.ds(n * CHUNK, CHUNK)
        swaps[n].wait_recv()
        tbuf[:, :, cols] = (
            pbuf[at.k, :, :, cols].astype(jnp.float32) + sbuf[:, :, cols].astype(jnp.float32)
        ).astype(jnp.bfloat16)
        for d in (2, 1, 3):
            copy = remote(
                tbuf.at[lax.rem(at.zh + d, 4), :, cols], zbuf.at[d - 1, :, cols],
                z_send.at[n, d], z_recv.at[n, d], at.dev(dzh=d),
            )
            copy.start()
            sums.append(copy)
    power = jnp.zeros((16, 1), jnp.float32)
    for n in range(CHUNKS):
        cols = pl.ds(n * CHUNK, CHUNK)
        for copy in sums[3 * n:3 * n + 3]:
            copy.wait_recv()
        total = pbuf[at.k, at.zh, :, cols].astype(jnp.float32) + sbuf[at.zh, :, cols].astype(jnp.float32)
        for d in range(3):
            total += zbuf[d, :, cols].astype(jnp.float32)
        total += res[:, cols].astype(jnp.float32)
        state_ref[:, cols] = total
        power += jnp.sum(total * total, axis=-1, keepdims=True)
    scale = lax.rsqrt(power / WIDTH + EPSILON)
    for n in range(CHUNKS):
        cols = pl.ds(n * CHUNK, CHUNK)
        normed_ref[:, cols] = (state_ref[:, cols] * scale * gain_ref[:, cols]).astype(jnp.bfloat16)

    for copy in kv + qs[1:] + swaps + sums:
        copy.wait_send()
    for j in range(1, 8):
        for copy in back(j):
            copy.wait_send()


def attention_call(query, keys, values, resid, norm_gain, out_weight):
    vmem, hbm = pl.BlockSpec(memory_space=pltpu.VMEM), pl.BlockSpec(memory_space=pl.ANY)
    bf, dma = jnp.bfloat16, pltpu.SemaphoreType.DMA
    return pl.pallas_call(
        attention_kernel,
        name="attention",
        out_shape=(jax.ShapeDtypeStruct((16, WIDTH), jnp.float32), jax.ShapeDtypeStruct((16, WIDTH), bf)),
        in_specs=[vmem, vmem, vmem, hbm, vmem, hbm],
        out_specs=(vmem, vmem),
        scratch_shapes=[
            pltpu.VMEM((4, 128, 256), bf), pltpu.VMEM((4, 128, 256), bf), pltpu.VMEM((8, 128, 256), bf),
            pltpu.VMEM((8, 256, 128), bf), pltpu.VMEM((8, 8, 128), jnp.float32),
            pltpu.VMEM((8, 256, 128), bf), pltpu.VMEM((8, 8, 128), jnp.float32),
            pltpu.VMEM((256, WIDTH), bf), pltpu.VMEM((16, WIDTH), bf), pltpu.VMEM((256, 128), bf),
            pltpu.VMEM((2, 4, 16, WIDTH), bf), pltpu.VMEM((4, 16, WIDTH), bf), pltpu.VMEM((4, 16, WIDTH), bf),
            pltpu.VMEM((3, 16, WIDTH), bf),
            dma((2, 4)), dma((2, 4)), dma((8,)), dma((8,)), dma((8,)), dma((8,)), dma((8,)), dma((8,)),
            dma((CHUNKS,)), dma((CHUNKS,)), dma((CHUNKS, 4)), dma((CHUNKS, 4)), dma((2,)),
        ],
        compiler_params=pltpu.CompilerParams(
            collective_id=1, has_side_effects=True, vmem_limit_bytes=40 << 20
        ),
    )(query, keys, values, resid, norm_gain.reshape(1, WIDTH), out_weight)


EXPERTS = 64
TOP = 6
CAP = 2

def slot_ranks(route_ids, text_rows):
    blocks, row_count, top_count = route_ids.shape
    flat = route_ids.reshape(blocks, row_count * top_count)
    usable = jnp.broadcast_to(text_rows[:, :, None], (blocks, row_count, top_count)).reshape(
        blocks, row_count * top_count
    )
    onehot = (flat[:, :, None] == jnp.arange(EXPERTS, dtype=jnp.int32)[None, None, :]) & usable[
        :, :, None
    ]
    counts = jnp.cumsum(onehot.astype(jnp.int32), axis=1)
    slot_rank = jnp.sum(jnp.where(onehot, counts, 0), axis=2) - 1
    return (
        slot_rank.reshape(blocks, row_count, top_count),
        usable.reshape(blocks, row_count, top_count),
    )


def expert_apply(batch, exp_gate, exp_up, exp_down):
    gate_part = jnp.einsum("clmd,ldf->clmf", batch, exp_gate, preferred_element_type=jnp.float32)
    up_part = jnp.einsum("clmd,ldf->clmf", batch, exp_up, preferred_element_type=jnp.float32)
    active = (jax.nn.silu(gate_part) * up_part).astype(jnp.bfloat16)
    return jnp.einsum(
        "clmf,lfd->clmd", active, exp_down, preferred_element_type=jnp.float32
    ).astype(jnp.bfloat16)


def body(
    query,
    keys,
    values,
    resid,
    flags,
    routes,
    gates,
    out_weight,
    norm_gain,
    img_gate,
    img_up,
    img_down,
    exp_gate,
    exp_up,
    exp_down,
):
    context_count = lax.axis_size("ctx")
    expert_count = lax.axis_size("exp")
    context_index = lax.axis_index("ctx")
    expert_index = lax.axis_index("exp")
    ctx_rows = query.shape[0]
    row_count = ctx_rows // expert_count
    model_width = resid.shape[1]
    state_own, normed_own = attention_call(query, keys, values, resid, norm_gain, out_weight)
    normed = lax.all_gather(normed_own, "exp", axis=0, tiled=True)
    own_start = expert_index * row_count
    image_gate, image_up, image_down = (
        lax.all_gather(img_gate, "exp", axis=0, tiled=True),
        lax.all_gather(img_up, "exp", axis=0, tiled=True),
        lax.all_gather(img_down, "exp", axis=0, tiled=True),
    )
    own_flags = lax.dynamic_slice_in_dim(flags, own_start, row_count, 0)
    portion = lax.all_gather(normed_own, "ctx", axis=0, tiled=True)
    gate_part = jnp.dot(portion, image_gate, preferred_element_type=jnp.float32)
    up_part = jnp.dot(portion, image_up, preferred_element_type=jnp.float32)
    image_act = (jax.nn.silu(gate_part) * up_part).astype(jnp.bfloat16)
    portion = image_act
    image_out = lax.psum_scatter(
        lax.dot_general(
            portion, image_down, (((1,), (1,)), ((), ())), preferred_element_type=jnp.float32
        ).astype(jnp.bfloat16),
        "ctx",
        scatter_dimension=0,
        tiled=True,
    ).astype(jnp.float32)
    split_count = max(1, context_count * expert_count // EXPERTS)
    group_count = EXPERTS // context_count
    local_count = exp_gate.shape[0]
    first_local = expert_index // split_count * local_count
    text_rows = flags == 0
    slot_rank, usable = slot_ranks(
        routes.reshape(expert_count, row_count, TOP), text_rows.reshape(expert_count, row_count)
    )
    slot_rank = slot_rank.reshape(ctx_rows, TOP)
    usable = usable.reshape(ctx_rows, TOP)
    subset = jnp.arange(ctx_rows, dtype=jnp.int32)[:, None] // row_count
    target = routes // group_count
    local_id = routes % group_count - first_local
    valid = usable & (local_id >= 0) & (local_id < local_count)
    slot_id = jnp.where(
        valid, ((target * local_count + local_id) * expert_count + subset) * CAP + slot_rank, -1
    )
    slot_total = context_count * local_count * expert_count * CAP
    matches = slot_id[None] == jnp.arange(slot_total, dtype=jnp.int32)[:, None, None]
    dispatch = jnp.any(matches, axis=-1).astype(jnp.bfloat16)
    weighting = jnp.sum(jnp.where(matches, gates[None].astype(jnp.float32), 0.0), axis=-1).astype(
        jnp.bfloat16
    )
    outgoing = jnp.dot(dispatch, normed, preferred_element_type=jnp.float32).astype(jnp.bfloat16)
    outgoing = outgoing.reshape(context_count, local_count, expert_count * CAP, model_width)
    returned = lax.all_to_all(
        expert_apply(
            lax.all_to_all(outgoing, "ctx", split_axis=0, concat_axis=0, tiled=True),
            exp_gate,
            exp_up,
            exp_down,
        ),
        "ctx",
        split_axis=0,
        concat_axis=0,
        tiled=True,
    )
    returned_flat = returned.reshape(slot_total, model_width)
    portion = weighting
    text_out = lax.psum_scatter(
        lax.dot_general(
            portion, returned_flat, (((0,), (0,)), ((), ())), preferred_element_type=jnp.float32
        ).astype(jnp.bfloat16),
        "exp",
        scatter_dimension=0,
        tiled=True,
    ).astype(jnp.float32)
    layer_out = state_own + jnp.where(own_flags[:, None] == 1, image_out, text_out)
    return layer_out.astype(jnp.bfloat16)


def solution(mesh):
    return jax.shard_map(
        body,
        mesh=mesh,
        in_specs=(
            P("ctx", "exp"),
            P("ctx", "exp"),
            P("ctx", "exp"),
            P("ctx", None),
            P("ctx"),
            P("ctx", None),
            P("ctx", None),
            P("exp", None),
            P(),
            P("exp", "ctx"),
            P("exp", "ctx"),
            P("exp", "ctx"),
            P(("ctx", "exp"), None, None),
            P(("ctx", "exp"), None, None),
            P(("ctx", "exp"), None, None),
        ),
        out_specs=P(("ctx", "exp"), None),
        check_vma=False,
    )
```

```python
import functools
import math

import jax
import jax.numpy as jnp
from jax import lax
from jax.experimental import pallas as pl
from jax.experimental.pallas import tpu as pltpu
from jax.sharding import PartitionSpec as P

MESH = pl.DeviceIdType.MESH
HEAD_DIM = 128
NEGATIVE = -1e30
EPSILON = 1e-05
WIDTH = 4096
CHUNK = 1024
CHUNKS = WIDTH // CHUNK


class Place:
    def __init__(self):
        c, e = lax.axis_index("ctx"), lax.axis_index("exp")
        self.c, self.e = c, e
        self.zl, self.x, self.y = lax.div(c, 16), lax.rem(lax.div(c, 4), 4), lax.rem(c, 4)
        self.zh, self.k = lax.div(e, 2), lax.rem(e, 2)
        self.z = self.zh * 2 + self.zl

    def dev(self, dx=0, dy=0, dzl=0, dzh=0, dk=0):
        x, y = lax.rem(self.x + dx + 4, 4), lax.rem(self.y + dy + 4, 4)
        zl, zh, k = lax.rem(self.zl + dzl, 2), lax.rem(self.zh + dzh + 4, 4), lax.rem(self.k + dk, 2)
        return (zl * 16 + x * 4 + y, zh * 2 + k)


def remote(src, dst, send, recv, device):
    return pltpu.make_async_remote_copy(
        src_ref=src, dst_ref=dst, send_sem=send, recv_sem=recv, device_id=device, device_id_type=MESH
    )


def attention_kernel(
    q_ref, k_ref, v_ref, resid_ref, gain_ref, ow_ref,
    state_ref, normed_ref,
    kbuf, vbuf, qbuf, obuf, stat, rbuf, rstat, ow, res, att, pbuf, sbuf, tbuf, zbuf,
    kv_send, kv_recv, q_send, q_recv, o_send, o_recv, s_send, s_recv, c_send, c_recv, z_send, z_recv, local_sem,
):
    at = Place()
    load_w = pltpu.make_async_copy(ow_ref, ow, local_sem.at[0])
    load_w.start()
    load_r = pltpu.make_async_copy(resid_ref.at[pl.ds(pl.multiple_of(at.e * 16, 16), 16)], res, local_sem.at[1])
    load_r.start()
    barrier = pltpu.get_barrier_semaphore()
    partners = [at.dev(dx=d) for d in (1, 2, 3)]
    partners += [at.dev(dzl=j // 4, dy=j % 4) for j in range(1, 8)]
    partners += [at.dev(dk=1)] + [at.dev(dzh=d) for d in (1, 2, 3)]
    for device in partners:
        pl.semaphore_signal(barrier, inc=1, device_id=device, device_id_type=MESH)
    kbuf[0] = k_ref[...]
    vbuf[0] = v_ref[...]
    qbuf[0] = q_ref[...]
    pl.semaphore_wait(barrier, len(partners))

    kv = []
    for d in (1, 2, 3):
        kv.append(remote(k_ref, kbuf.at[d], kv_send.at[0, d], kv_recv.at[0, d], at.dev(dx=d)))
        kv.append(remote(v_ref, vbuf.at[d], kv_send.at[1, d], kv_recv.at[1, d], at.dev(dx=d)))
    qs = [None] + [
        remote(q_ref, qbuf.at[j], q_send.at[j], q_recv.at[j], at.dev(dzl=j // 4, dy=j % 4)) for j in range(1, 8)
    ]
    for j in range(1, 8):
        qs[j].start()
    for copy in kv:
        copy.start()

    rows = lax.broadcasted_iota(jnp.int32, (512, 128), 0)
    lanes = lax.broadcasted_iota(jnp.int32, (512, 128), 1)
    from_x = lax.rem(at.x - lax.div(rows, 128) + 4, 4)
    key_spot = (at.zl * 16 + from_x * 4 + at.y) * 128 + lax.rem(rows, 128) - lanes
    for copy in kv:
        copy.wait_recv()

    def back(j):
        device = at.dev(dzl=lax.div(j, 4), dy=4 - lax.rem(j, 4))
        return (
            remote(obuf.at[j], rbuf.at[j], o_send.at[j], o_recv.at[j], device),
            remote(stat.at[j], rstat.at[j], s_send.at[j], s_recv.at[j], device),
        )

    def one_block(j, _):
        @pl.when(j > 0)
        def _():
            remote(q_ref, qbuf.at[j], q_send.at[j], q_recv.at[j], at.dev(dzl=lax.div(j, 4), dy=lax.rem(j, 4))).wait_recv()

        q_zl = lax.rem(at.zl + lax.div(j, 4), 2)
        q_y = lax.rem(at.y + 4 - lax.rem(j, 4), 4)
        limit = (q_zl * 16 + at.x * 4 + q_y) * 128
        allowed = key_spot <= limit
        stats = []
        for h in range(2):
            cols = slice(h * HEAD_DIM, (h + 1) * HEAD_DIM)
            kh = kbuf[:, :, cols].reshape(512, HEAD_DIM)
            vh = vbuf[:, :, cols].reshape(512, HEAD_DIM)
            qh = qbuf[j, :, cols]
            s = lax.dot_general(kh, qh, (((1,), (1,)), ((), ())), preferred_element_type=jnp.float32)
            s = jnp.where(allowed, s * (1.0 / math.sqrt(HEAD_DIM)), NEGATIVE)
            m = jnp.max(s, axis=0, keepdims=True)
            p = jnp.where(allowed, jnp.exp(s - m), 0.0)
            l = jnp.sum(p, axis=0, keepdims=True)
            o = lax.dot_general(vh, p.astype(jnp.bfloat16), (((0,), (0,)), ((), ())), preferred_element_type=jnp.float32)
            obuf[j, cols, :] = o.astype(jnp.bfloat16)
            stats += [m, l]
        stat[j] = jnp.concatenate(stats + stats, axis=0)

        @pl.when(j > 0)
        def _():
            for copy in back(j):
                copy.start()

        return 0

    lax.fori_loop(0, 8, one_block, 0)
    rbuf[0] = obuf[0]
    rstat[0] = stat[0]
    for j in range(1, 8):
        for copy in back(j):
            copy.wait_recv()
    for h in range(2):
        cols = slice(h * HEAD_DIM, (h + 1) * HEAD_DIM)
        top = rstat[0, 2 * h:2 * h + 1, :]
        for j in range(1, 8):
            top = jnp.maximum(top, rstat[j, 2 * h:2 * h + 1, :])
        total = jnp.zeros((HEAD_DIM, 128), jnp.float32)
        denom = jnp.zeros((1, 128), jnp.float32)
        for j in range(8):
            w = jnp.exp(rstat[j, 2 * h:2 * h + 1, :] - top)
            denom += w * rstat[j, 2 * h + 1:2 * h + 2, :]
            total += w * rbuf[j, cols, :].astype(jnp.float32)
        att[cols, :] = (total / denom).astype(jnp.bfloat16)

    load_w.wait()
    load_r.wait()
    swaps, sums = [], []
    for n in range(CHUNKS):
        cols = pl.ds(n * CHUNK, CHUNK)
        part = lax.dot_general(
            att[...], ow[:, cols], (((0,), (0,)), ((), ())), preferred_element_type=jnp.float32
        ).astype(jnp.bfloat16)
        for b in range(8):
            pbuf[b % 2, b // 2, :, cols] = part[16 * b:16 * b + 16]
        copy = remote(pbuf.at[1 - at.k, :, :, cols], sbuf.at[:, :, cols], c_send.at[n], c_recv.at[n], at.dev(dk=1))
        copy.start()
        swaps.append(copy)
    for n in range(CHUNKS):
        cols = pl.ds(n * CHUNK, CHUNK)
        swaps[n].wait_recv()
        tbuf[:, :, cols] = (
            pbuf[at.k, :, :, cols].astype(jnp.float32) + sbuf[:, :, cols].astype(jnp.float32)
        ).astype(jnp.bfloat16)
        for d in (2, 1, 3):
            copy = remote(
                tbuf.at[lax.rem(at.zh + d, 4), :, cols], zbuf.at[d - 1, :, cols],
                z_send.at[n, d], z_recv.at[n, d], at.dev(dzh=d),
            )
            copy.start()
            sums.append(copy)
    power = jnp.zeros((16, 1), jnp.float32)
    for n in range(CHUNKS):
        cols = pl.ds(n * CHUNK, CHUNK)
        for copy in sums[3 * n:3 * n + 3]:
            copy.wait_recv()
        total = pbuf[at.k, at.zh, :, cols].astype(jnp.float32) + sbuf[at.zh, :, cols].astype(jnp.float32)
        for d in range(3):
            total += zbuf[d, :, cols].astype(jnp.float32)
        total += res[:, cols].astype(jnp.float32)
        state_ref[:, cols] = total
        power += jnp.sum(total * total, axis=-1, keepdims=True)
    scale = lax.rsqrt(power / WIDTH + EPSILON)
    for n in range(CHUNKS):
        cols = pl.ds(n * CHUNK, CHUNK)
        normed_ref[:, cols] = (state_ref[:, cols] * scale * gain_ref[:, cols]).astype(jnp.bfloat16)

    for copy in kv + qs[1:] + swaps + sums:
        copy.wait_send()
    for j in range(1, 8):
        for copy in back(j):
            copy.wait_send()


def attention_call(query, keys, values, resid, norm_gain, out_weight):
    vmem, hbm = pl.BlockSpec(memory_space=pltpu.VMEM), pl.BlockSpec(memory_space=pl.ANY)
    bf, dma = jnp.bfloat16, pltpu.SemaphoreType.DMA
    return pl.pallas_call(
        attention_kernel,
        name="attention",
        out_shape=(jax.ShapeDtypeStruct((16, WIDTH), jnp.float32), jax.ShapeDtypeStruct((16, WIDTH), bf)),
        in_specs=[vmem, vmem, vmem, hbm, vmem, hbm],
        out_specs=(vmem, vmem),
        scratch_shapes=[
            pltpu.VMEM((4, 128, 256), bf), pltpu.VMEM((4, 128, 256), bf), pltpu.VMEM((8, 128, 256), bf),
            pltpu.VMEM((8, 256, 128), bf), pltpu.VMEM((8, 8, 128), jnp.float32),
            pltpu.VMEM((8, 256, 128), bf), pltpu.VMEM((8, 8, 128), jnp.float32),
            pltpu.VMEM((256, WIDTH), bf), pltpu.VMEM((16, WIDTH), bf), pltpu.VMEM((256, 128), bf),
            pltpu.VMEM((2, 4, 16, WIDTH), bf), pltpu.VMEM((4, 16, WIDTH), bf), pltpu.VMEM((4, 16, WIDTH), bf),
            pltpu.VMEM((3, 16, WIDTH), bf),
            dma((2, 4)), dma((2, 4)), dma((8,)), dma((8,)), dma((8,)), dma((8,)), dma((8,)), dma((8,)),
            dma((CHUNKS,)), dma((CHUNKS,)), dma((CHUNKS, 4)), dma((CHUNKS, 4)), dma((2,)),
        ],
        compiler_params=pltpu.CompilerParams(
            collective_id=1, has_side_effects=True, vmem_limit_bytes=40 << 20
        ),
    )(query, keys, values, resid, norm_gain.reshape(1, WIDTH), out_weight)


def ring(at, dz, dk=0):
    z = lax.rem(at.z + dz + 8, 8)
    return (lax.rem(z, 2) * 16 + at.x * 4 + at.y, lax.div(z, 2) * 2 + lax.rem(at.k + dk, 2))


def selection(at, meta, send_map, back_map):
    lane = lax.broadcasted_iota(jnp.int32, (16, 128), 1)
    spot = lax.broadcasted_iota(jnp.int32, (16, 128), 0)
    to_x = lax.rem(at.x + lax.div(spot, 4), 4)
    to_y = lax.rem(at.y + lax.rem(spot, 4), 4)
    expert = (2 * (at.zl * 16 + to_x * 4 + to_y) + lax.div(at.zh, 2)).astype(jnp.float32)
    chosen = jnp.zeros((16, 128), jnp.float32)
    gate = jnp.zeros((16, 128), jnp.float32)
    for j in range(6):
        hit = jnp.where(meta[j:j + 1, :] == expert, 1.0, 0.0)
        chosen += hit
        gate += hit * meta[6 + j:7 + j, :]
    image = jnp.broadcast_to(meta[12:13, :], (16, 128))
    chosen = jnp.where(image == 0.0, chosen, 0.0)
    gate = jnp.where(image == 0.0, gate, 0.0)
    row = lax.broadcasted_iota(jnp.int32, (128, 128), 0)
    col = lax.broadcasted_iota(jnp.int32, (128, 128), 1)
    earlier = jnp.where((lax.div(row, 16) == lax.div(col, 16)) & (row < col), 1.0, 0.0).astype(jnp.bfloat16)
    rank = jnp.dot(
        jnp.concatenate([chosen, image], axis=0).astype(jnp.bfloat16), earlier, preferred_element_type=jnp.float32
    )
    sub = lax.div(lane, 16)
    text_slot = (2 * sub).astype(jnp.float32) + rank[0:16]
    text_slot = jnp.where(chosen > 0.0, text_slot, -1.0)
    mine = (image > 0.0) & (lax.div(sub, 2) == at.zh)
    image_slot = jnp.where(mine, (8 * (sub - 2 * at.zh)).astype(jnp.float32) + rank[16:32], -1.0)
    slot = spot.astype(jnp.float32)
    image_map = jnp.where(image_slot == slot, 1.0, 0.0).astype(jnp.bfloat16)
    for t in range(16):
        match = text_slot[t:t + 1, :] == slot
        send_map[t, 0:16, :] = jnp.where(match, 1.0, 0.0).astype(jnp.bfloat16)
        send_map[t, 16:32, :] = image_map
        back_map[t, 0:16, :] = jnp.where(match, gate[t:t + 1, :], 0.0).astype(jnp.bfloat16)
        back_map[t, 16:32, :] = image_map


def active(gate, up):
    return (gate / (1.0 + jnp.exp(-gate)) * up).astype(jnp.bfloat16)


def nt_dot(a, b):
    return lax.dot_general(a, b, (((1,), (1,)), ((), ())), preferred_element_type=jnp.float32)


def ffn_kernel(
    normed_ref, state_ref, meta_ref, eg_ref, eu_ref, ed_ref, iw_ref,
    out_ref,
    wg, wu, wd, wi, other, send_map, back_map, rows, dsend, xs, acc, ysend, ys, zsum, zsend, zrecv, tail_send, tail_recv,
    w_send, w_recv, w_local, m_send, m_recv, p_send, p_recv, r_send, r_recv, d_send, d_recv,
    i_send, i_recv, f_send, f_recv, t_send, t_recv, y_send, y_recv, e_send, e_recv, l_send, l_recv,
):
    at = Place()
    z, k, zh = at.z, at.k, at.zh
    p = lax.rem(at.zl + k, 2)
    s = 1 - 2 * k
    even, odd = p == 0, p == 1
    chunk = [pl.ds(n * CHUNK, CHUNK) for n in range(CHUNKS)]
    pending = []

    weights = []
    for i, (src, dst) in enumerate(((eg_ref, wg), (eu_ref, wu), (ed_ref, wd))):
        copy = pltpu.make_async_copy(src.at[0], dst.at[0], w_local.at[i])
        copy.start()
        weights.append(copy)
    barrier = pltpu.get_barrier_semaphore()
    partners = [at.dev(dk=1), ring(at, 1), ring(at, 7)] + [at.dev(dzh=d) for d in (1, 2, 3)]
    partners += [at.dev(dx=t // 4, dy=t % 4) for t in range(1, 16)]
    for device in partners:
        pl.semaphore_signal(barrier, inc=1, device_id=device, device_id_type=MESH)
    wi[at.e] = iw_ref[...]
    pl.semaphore_wait(barrier, len(partners))

    meta_copy = remote(meta_ref, other, m_send, m_recv, at.dev(dzl=1))
    meta_copy.start()

    def pair_copy(n):
        return remote(
            normed_ref.at[:, chunk[n]], rows.at[zh, k, :, chunk[n]], p_send.at[n], p_recv.at[n], at.dev(dk=1)
        )

    def pair_arrival(n):
        return remote(
            normed_ref.at[:, chunk[n]], rows.at[zh, 1 - k, :, chunk[n]], p_send.at[n], p_recv.at[n], at.dev(dk=1)
        )

    def ring_copy(side, i, n):
        step = (2 * i + p) * s
        origin = lax.rem(z - step + 16, 8) if side == 0 else lax.rem(z + step + 16, 8)
        part = rows.at[lax.div(origin, 2), :, :, chunk[n]]
        return remote(part, part, r_send.at[side, i, n], r_recv.at[side, i, n], ring(at, s if side == 0 else -s))

    def ring_arrival(side, i, n):
        step = (2 * i + 2 - p) * s
        origin = lax.rem(z - step + 16, 8) if side == 0 else lax.rem(z + step + 16, 8)
        part = rows.at[lax.div(origin, 2), :, :, chunk[n]]
        return remote(part, part, r_send.at[side, i, n], r_recv.at[side, i, n], ring(at, s if side == 0 else -s))

    def plane(t, back=False):
        dx, dy = lax.div(t, 4), lax.rem(t, 4)
        return at.dev(dx=4 - dx, dy=4 - dy) if back else at.dev(dx=dx, dy=dy)

    def row_copy(t, n):
        return remote(dsend.at[t, :, chunk[n]], xs.at[t, :, chunk[n]], d_send.at[t, n], d_recv.at[t, n], plane(t))

    @pl.when(odd)
    def _():
        for n in range(CHUNKS):
            pair_copy(n).start()

    @pl.when(even)
    def _():
        rows[zh, k] = normed_ref[...]

    def stage_0(n):
        @pl.when(even)
        def _():
            pair_arrival(n).wait_recv()
            ring_copy(0, 0, n).start()
            ring_copy(1, 0, n).start()

    def stage_1(n):
        for side in range(2):
            ring_arrival(side, 0, n).wait_recv()

            @pl.when(even)
            def _():
                ring_copy(side, 1, n).start()

            @pl.when(odd)
            def _():
                ring_copy(side, 0, n).start()

    def stage_2(n):
        ring_arrival(0, 1, n).wait_recv()

        @pl.when(odd)
        def _():
            ring_copy(0, 1, n).start()
            ring_arrival(1, 1, n).wait_recv()

    def stage_3(n):
        part = rows[:, :, :, chunk[n]].reshape(128, CHUNK)
        picked = jnp.dot(
            send_map[...].reshape(512, 128), part, preferred_element_type=jnp.float32
        ).astype(jnp.bfloat16).reshape(16, 32, CHUNK)
        dsend[:, :, chunk[n]] = picked
        xs[0, :, chunk[n]] = picked[0]

        def go(t, _):
            row_copy(t, n).start()
            return 0

        lax.fori_loop(1, 16, go, 0)

    stage_0(0)
    meta_copy.wait_recv()
    selection(at, jnp.where(even, meta_ref[...], other[...]), send_map, back_map)
    for step in range(1, CHUNKS + 3):
        if step < CHUNKS:
            stage_0(step)
        if 0 <= step - 1 < CHUNKS:
            stage_1(step - 1)
        if 0 <= step - 2 < CHUNKS:
            stage_2(step - 2)
            stage_3(step - 2)
    for i, (src, dst) in enumerate(((eg_ref, wg), (eu_ref, wu), (ed_ref, wd))):
        copy = remote(src.at[0], dst.at[1], w_send.at[i], w_recv.at[i], at.dev(dk=1))
        copy.start()
        pending.append(copy)
    swap = pending[:]

    own = wi.at[at.e]
    image_copies = [remote(own, own, i_send.at[0], i_recv.at[0], at.dev(dk=1))]
    image_copies += [remote(own, own, i_send.at[d], i_recv.at[d], at.dev(dzh=d)) for d in (1, 2, 3)]
    for copy in image_copies:
        copy.start()

    def image_piece(origin):
        return wi.at[origin]

    def image_arrival(d):
        part = wi.at[2 * lax.rem(zh + 4 - d, 4) + k]
        return remote(part, part, i_send.at[d], i_recv.at[d], at.dev(dzh=d))

    def image_pass(d):
        part = wi.at[2 * lax.rem(zh + 4 - d, 4) + k]
        return remote(part, part, f_send.at[d], f_recv.at[d], at.dev(dk=1))

    def image_pass_arrival(d):
        part = wi.at[2 * lax.rem(zh + 4 - d, 4) + 1 - k]
        return remote(part, part, f_send.at[d], f_recv.at[d], at.dev(dk=1))

    for copy in weights[:2]:
        copy.wait()
    for copy in swap[:2]:
        copy.wait_recv()
    for n in range(CHUNKS):
        def arrive(t, _):
            row_copy(t, n).wait_recv()
            return 0

        lax.fori_loop(1, 16, arrive, 0)
        part = xs[:, 0:16, chunk[n]].reshape(256, CHUNK)
        for q in range(2):
            for i, w in enumerate((wg, wu)):
                term = jnp.dot(part, w[q, n * CHUNK:(n + 1) * CHUNK, :], preferred_element_type=jnp.float32)
                if n == 0:
                    acc[q, i] = term
                else:
                    acc[q, i] += term
    acts = [active(acc[q, 0], acc[q, 1]) for q in range(2)]
    weights[2].wait()
    swap[2].wait_recv()

    def text_back(t, n):
        return remote(
            ysend.at[t, 0:16, chunk[n]], ys.at[t, 0:16, chunk[n]], t_send.at[t, n], t_recv.at[t, n], plane(t, True)
        )

    def image_back(t, n):
        return remote(
            ysend.at[t, 16:32, chunk[n]], ys.at[t, 16:32, chunk[n]], y_send.at[t, n], y_recv.at[t, n], plane(t, True)
        )

    def send_back(result, low, n, copy):
        result = result.astype(jnp.bfloat16).reshape(16, 16, CHUNK)
        ysend[:, low:low + 16, chunk[n]] = result
        ys[0, low:low + 16, chunk[n]] = result[0]

        def go(t, _):
            copy(t, n).start()
            return 0

        lax.fori_loop(1, 16, go, 0)

    for n in range(CHUNKS):
        result = jnp.dot(acts[0], wd[0, :, chunk[n]], preferred_element_type=jnp.float32)
        result += jnp.dot(acts[1], wd[1, :, chunk[n]], preferred_element_type=jnp.float32)
        send_back(result, 0, n, text_back)

    for d in (1, 3, 2):
        image_arrival(d).wait_recv()
        image_pass(d).start()
    remote(own, wi.at[2 * zh + 1 - k], i_send.at[0], i_recv.at[0], at.dev(dk=1)).wait_recv()
    for d in (1, 3, 2):
        image_pass_arrival(d).wait_recv()
    gate = jnp.zeros((256, 176), jnp.float32)
    up = jnp.zeros((256, 176), jnp.float32)
    for e in range(8):
        part = xs[:, 16:32, e * 512:(e + 1) * 512].reshape(256, 512)
        gate += nt_dot(part, wi[e, 0])
        up += nt_dot(part, wi[e, 1])
    image_act = active(gate, up)
    for n in range(CHUNKS):
        result = jnp.concatenate(
            [jnp.dot(image_act, wi[e, 2], preferred_element_type=jnp.float32) for e in (2 * n, 2 * n + 1)], axis=1
        )
        send_back(result, 16, n, image_back)

    def sum_copy(side, i, n):
        return remote(
            zsend.at[side, i, :, chunk[n]], zrecv.at[side, i, :, chunk[n]],
            e_send.at[side, i, n], e_recv.at[side, i, n], ring(at, -s if side == 0 else s),
        )

    def pass_sum(side, i, n, distance, arrival):
        step = distance * s
        target = lax.div(lax.rem(z - step + 16, 8) if side == 0 else lax.rem(z + step + 16, 8), 2)
        value = zsum[target, :, chunk[n]]
        if arrival is not None:
            sum_copy(side, arrival, n).wait_recv()
            value += zrecv[side, arrival, :, chunk[n]].astype(jnp.float32)
        zsend[side, i, :, chunk[n]] = value.astype(jnp.bfloat16)
        sum_copy(side, i, n).start()

    def tail_copy(n):
        return remote(tail_send.at[:, chunk[n]], tail_recv.at[:, chunk[n]], l_send.at[n], l_recv.at[n], at.dev(dk=1))

    def end_0(n):
        def arrive(t, _):
            text_back(t, n).wait_recv()
            image_back(t, n).wait_recv()
            return 0

        lax.fori_loop(1, 16, arrive, 0)
        total = lax.dot_general(
            back_map[...].reshape(512, 128), ys[:, :, chunk[n]].reshape(512, CHUNK),
            (((0,), (0,)), ((), ())), preferred_element_type=jnp.float32,
        )
        zsum[:, :, chunk[n]] = total.reshape(4, 32, CHUNK)

        @pl.when(even)
        def _():
            pass_sum(0, 0, n, 4, None)

        @pl.when(odd)
        def _():
            pass_sum(1, 0, n, 3, None)

    def end_1(n):
        @pl.when(odd)
        def _():
            pass_sum(0, 0, n, 3, 0)

        @pl.when(even)
        def _():
            pass_sum(1, 1, n, 2, 0)

    def end_2(n):
        @pl.when(even)
        def _():
            pass_sum(0, 1, n, 2, 0)

        @pl.when(odd)
        def _():
            pass_sum(1, 1, n, 1, 1)

    def end_3(n):
        @pl.when(odd)
        def _():
            pass_sum(0, 1, n, 1, 1)

    def end_4(n):
        @pl.when(even)
        def _():
            sum_copy(0, 1, n).wait_recv()
            sum_copy(1, 1, n).wait_recv()
            total = zsum[zh, :, chunk[n]] + zrecv[0, 1, :, chunk[n]].astype(jnp.float32)
            total += zrecv[1, 1, :, chunk[n]].astype(jnp.float32)
            first, second = total[0:16], total[16:32]
            tail_send[:, chunk[n]] = jnp.where(k == 0, second, first).astype(jnp.bfloat16)
            tail_copy(n).start()
            mine = jnp.where(k == 0, first, second)
            out_ref[:, chunk[n]] = (state_ref[:, chunk[n]] + mine).astype(jnp.bfloat16)

    def end_5(n):
        @pl.when(odd)
        def _():
            tail_copy(n).wait_recv()
            out_ref[:, chunk[n]] = (
                state_ref[:, chunk[n]] + tail_recv[:, chunk[n]].astype(jnp.float32)
            ).astype(jnp.bfloat16)

    ends = (end_0, end_1, end_2, end_3, end_4, end_5)
    for step in range(CHUNKS + len(ends) - 1):
        for i, end in enumerate(ends):
            if 0 <= step - i < CHUNKS:
                end(step - i)

    meta_copy.wait_send()
    for copy in pending + image_copies:
        copy.wait_send()
    for d in (1, 2, 3):
        image_pass(d).wait_send()
    for n in range(CHUNKS):
        def sent(t, _):
            row_copy(t, n).wait_send()
            text_back(t, n).wait_send()
            image_back(t, n).wait_send()
            return 0

        lax.fori_loop(1, 16, sent, 0)

        @pl.when(even)
        def _():
            for side, i in ((0, 0), (1, 0), (0, 1), (1, 1)):
                ring_copy(side, i, n).wait_send()
            for side, i in ((0, 0), (0, 1), (1, 1)):
                sum_copy(side, i, n).wait_send()
            tail_copy(n).wait_send()

        @pl.when(odd)
        def _():
            pair_copy(n).wait_send()
            for side, i in ((0, 0), (1, 0), (0, 1)):
                ring_copy(side, i, n).wait_send()
            for side, i in ((0, 0), (1, 0), (0, 1), (1, 1)):
                sum_copy(side, i, n).wait_send()


def ffn_call(normed, state, meta, exp_gate, exp_up, exp_down, image_weights):
    vmem, hbm = pl.BlockSpec(memory_space=pltpu.VMEM), pl.BlockSpec(memory_space=pl.ANY)
    bf, dma = jnp.bfloat16, pltpu.SemaphoreType.DMA
    two = [dma((16, CHUNKS)), dma((16, CHUNKS))]
    return pl.pallas_call(
        ffn_kernel,
        name="feed_forward",
        out_shape=jax.ShapeDtypeStruct((16, WIDTH), bf),
        in_specs=[vmem, vmem, vmem, hbm, hbm, hbm, vmem],
        out_specs=vmem,
        scratch_shapes=[
            pltpu.VMEM((2, WIDTH, 352), bf), pltpu.VMEM((2, WIDTH, 352), bf), pltpu.VMEM((2, 352, WIDTH), bf),
            pltpu.VMEM((8, 3, 176, 512), bf), pltpu.VMEM((16, 128), jnp.float32),
            pltpu.VMEM((16, 32, 128), bf), pltpu.VMEM((16, 32, 128), bf),
            pltpu.VMEM((4, 2, 16, WIDTH), bf), pltpu.VMEM((16, 32, WIDTH), bf), pltpu.VMEM((16, 32, WIDTH), bf),
            pltpu.VMEM((2, 2, 256, 352), jnp.float32),
            pltpu.VMEM((16, 32, WIDTH), bf), pltpu.VMEM((16, 32, WIDTH), bf),
            pltpu.VMEM((4, 32, WIDTH), jnp.float32),
            pltpu.VMEM((2, 2, 32, WIDTH), bf), pltpu.VMEM((2, 2, 32, WIDTH), bf),
            pltpu.VMEM((16, WIDTH), bf), pltpu.VMEM((16, WIDTH), bf),
            dma((3,)), dma((3,)), dma((3,)), dma, dma, dma((CHUNKS,)), dma((CHUNKS,)),
            dma((2, 2, CHUNKS)), dma((2, 2, CHUNKS)), *two,
            dma((4,)), dma((4,)), dma((4,)), dma((4,)), *two, *two,
            dma((2, 2, CHUNKS)), dma((2, 2, CHUNKS)), dma((CHUNKS,)), dma((CHUNKS,)),
        ],
        compiler_params=pltpu.CompilerParams(
            collective_id=2, has_side_effects=True, vmem_limit_bytes=56 << 20
        ),
    )(normed, state, meta, exp_gate, exp_up, exp_down, image_weights)


def body(
    query, keys, values, resid, flags, routes, gates, out_weight, norm_gain,
    img_gate, img_up, img_down, exp_gate, exp_up, exp_down,
):
    meta = jnp.concatenate(
        [routes.astype(jnp.float32), gates.astype(jnp.float32), flags.astype(jnp.float32)[:, None],
         jnp.zeros((flags.shape[0], 3), jnp.float32)], axis=1,
    ).T
    image_weights = jnp.pad(jnp.stack([img_gate.T, img_up.T, img_down.T]), ((0, 0), (0, 4), (0, 0)))
    state, normed = attention_call(query, keys, values, resid, norm_gain, out_weight)
    return ffn_call(normed, state, meta, exp_gate, exp_up, exp_down, image_weights)


def solution(mesh):
    return jax.shard_map(
        body,
        mesh=mesh,
        in_specs=(
            P("ctx", "exp"),
            P("ctx", "exp"),
            P("ctx", "exp"),
            P("ctx", None),
            P("ctx"),
            P("ctx", None),
            P("ctx", None),
            P("exp", None),
            P(),
            P("exp", "ctx"),
            P("exp", "ctx"),
            P("exp", "ctx"),
            P(("ctx", "exp"), None, None),
            P(("ctx", "exp"), None, None),
            P(("ctx", "exp"), None, None),
        ),
        out_specs=P(("ctx", "exp"), None),
        check_vma=False,
    )
```

```python
import math

import jax
import jax.numpy as jnp
from jax import lax
from jax.experimental import pallas as pl
from jax.experimental.pallas import tpu as pltpu
from jax.sharding import PartitionSpec as P

MESH = pl.DeviceIdType.MESH
HEAD_DIM = 128
NEGATIVE = -1e30
EPSILON = 1e-05
WIDTH = 4096
CHUNK = 1024
CHUNKS = WIDTH // CHUNK
BF16 = jnp.bfloat16
F32 = jnp.float32


class Place:
    def __init__(self):
        c, e = lax.axis_index("ctx"), lax.axis_index("exp")
        self.e = e
        self.zl, self.x, self.y = lax.div(c, 16), lax.rem(lax.div(c, 4), 4), lax.rem(c, 4)
        self.zh, self.k = lax.div(e, 2), lax.rem(e, 2)
        self.z = self.zh * 2 + self.zl

    def dev(self, dx=0, dy=0, dzl=0, dzh=0, dk=0):
        x, y = lax.rem(self.x + dx + 4, 4), lax.rem(self.y + dy + 4, 4)
        zl, zh, k = lax.rem(self.zl + dzl, 2), lax.rem(self.zh + dzh + 4, 4), lax.rem(self.k + dk, 2)
        return (zl * 16 + x * 4 + y, zh * 2 + k)

    def column(self, dz, core):
        z = lax.rem(self.z + dz, 8)
        return (lax.rem(z, 2) * 16 + self.x * 4 + self.y, lax.div(z, 2) * 2 + core)

    def plane(self, t, back=False):
        dx, dy = lax.div(t, 4), lax.rem(t, 4)
        return self.dev(dx=4 - dx, dy=4 - dy) if back else self.dev(dx=dx, dy=dy)


def remote(src, dst, send, recv, device):
    return pltpu.make_async_remote_copy(
        src_ref=src, dst_ref=dst, send_sem=send, recv_sem=recv, device_id=device, device_id_type=MESH
    )


def nt_dot(a, b):
    return lax.dot_general(a, b, (((1,), (1,)), ((), ())), preferred_element_type=F32)


def tn_dot(a, b):
    return lax.dot_general(a, b, (((0,), (0,)), ((), ())), preferred_element_type=F32)


def pieces(value):
    first = value.astype(BF16).astype(F32)
    second = (value - first).astype(BF16).astype(F32)
    return [first, second, value - first - second]


def active(gate, up):
    return (gate / (1.0 + jnp.exp(-gate)) * up).astype(BF16)


def each(low, high, step):
    def go(t, carried):
        step(t)
        return carried

    lax.fori_loop(low, high, go, 0)


def selection(at, meta, text_map, back_map, image_map):
    lane = lax.broadcasted_iota(jnp.int32, (16, 128), 1)
    spot = lax.broadcasted_iota(jnp.int32, (16, 128), 0)
    to_x = lax.rem(at.x + lax.div(spot, 4), 4)
    to_y = lax.rem(at.y + lax.rem(spot, 4), 4)
    expert = (2 * (at.zl * 16 + to_x * 4 + to_y) + lax.div(at.zh, 2)).astype(F32)
    chosen = jnp.zeros((16, 128), F32)
    gate = jnp.zeros((16, 128), F32)
    for j in range(6):
        hit = jnp.where(meta[j:j + 1, :] == expert, 1.0, 0.0)
        chosen += hit
        gate += hit * meta[6 + j:7 + j, :]
    image = jnp.broadcast_to(meta[12:13, :], (16, 128))
    chosen = jnp.where(image == 0.0, chosen, 0.0)
    gate = jnp.where(image == 0.0, gate, 0.0)
    row = lax.broadcasted_iota(jnp.int32, (128, 128), 0)
    col = lax.broadcasted_iota(jnp.int32, (128, 128), 1)
    earlier = jnp.where((lax.div(row, 16) == lax.div(col, 16)) & (row < col), 1.0, 0.0).astype(BF16)
    rank = jnp.dot(jnp.concatenate([chosen, image], axis=0).astype(BF16), earlier, preferred_element_type=F32)
    sub = lax.div(lane, 16)
    text_slot = jnp.where(chosen > 0.0, (2 * sub).astype(F32) + rank[0:16], -1.0)
    mine = (image > 0.0) & (lax.div(sub, 2) == at.zh)
    image_slot = jnp.where(mine, (8 * (sub - 2 * at.zh)).astype(F32) + rank[16:32], -1.0)
    slot = spot.astype(F32)
    image_map[...] = jnp.where(image_slot == slot, 1.0, 0.0).astype(BF16)
    for t in range(16):
        match = text_slot[t:t + 1, :] == slot
        text_map[16 * t:16 * t + 16, :] = jnp.where(match, 1.0, 0.0).astype(BF16)
        back_map[16 * t:16 * t + 16, :] = jnp.where(match, gate[t:t + 1, :], 0.0).astype(BF16)


def layer_kernel(
    q_ref, k_ref, v_ref, resid_ref, flags_ref, routes_ref, gates_ref, ow_ref, gain_ref,
    ig_ref, iu_ref, id_ref, eg_ref, eu_ref, ed_ref,
    out_ref,
    kbuf, vbuf, qbuf, obuf, rbuf, ow, res, att, pbuf, sbuf, tbuf, zbuf, state, normed,
    wg, wu, wd, wi, meta, other, text_map, back_map, image_map, rows, tsend, xt, xi, acc,
    ysend, ys, isend, ir1, is2, ir2, zsend, zrecv, zown,
    kv_send, kv_recv, q_send, q_recv, o_send, o_recv, c_send, c_recv, z_send, z_recv, local_sem,
    w_send, w_recv, m_send, m_recv, g_send, g_recv, d_send, d_recv, x1_send, x1_recv, x2_send, x2_recv,
    i_send, i_recv, f_send, f_recv, t_send, t_recv, y1_send, y1_recv, y2_send, y2_recv, e_send, e_recv,
):
    at = Place()
    z, k, zh, zl = at.z, at.k, at.zh, at.zl
    p = lax.rem(zl + k, 2)
    even, odd = p == 0, p == 1
    chunk = [pl.ds(n * CHUNK, CHUNK) for n in range(CHUNKS)]
    heads = [pl.ds(h * HEAD_DIM, HEAD_DIM) for h in range(2)]

    def load(i, src, dst):
        copy = pltpu.make_async_copy(src, dst, local_sem.at[i])
        copy.start()
        return copy

    own_kv = []
    for h in range(2):
        own_kv.append([
            load(3 * h, q_ref.at[:, heads[h]], qbuf.at[h, 0]),
            load(3 * h + 1, k_ref.at[:, heads[h]], kbuf.at[h, 0]),
            load(3 * h + 2, v_ref.at[:, heads[h]], vbuf.at[h, 0]),
        ])
    own_rows = pl.ds(pl.multiple_of(at.e * 16, 16), 16)
    load_r = load(6, resid_ref.at[own_rows], res)
    load_w = load(7, ow_ref, ow)
    barrier = pltpu.get_barrier_semaphore()
    partners = [at.plane(t) for t in range(1, 16)]
    partners += [at.column(dz, lax.rem(k + dk, 2)) for dz in range(8) for dk in range(2) if (dz, dk) != (0, 0)]
    partners += [at.dev(dzl=1, dy=d) for d in (1, 2, 3)]
    for device in partners:
        pl.semaphore_signal(barrier, inc=1, device_id=device, device_id_type=MESH)
    meta[0:6, :] = routes_ref[...].astype(F32)
    meta[6:12, :] = gates_ref[...].astype(F32)
    meta[12:16, :] = jnp.broadcast_to(flags_ref[...].astype(F32), (4, 128))
    pad = jnp.zeros((4, 512), BF16)
    for i, ref in enumerate((ig_ref, iu_ref, id_ref)):
        wi[at.e, i] = jnp.concatenate([ref[...], pad], axis=0)
    pl.semaphore_wait(barrier, len(partners))

    def q_copy(h, j):
        dy, dzl = lax.rem(j, 4), lax.div(j, 4)
        return remote(q_ref.at[:, heads[h]], qbuf.at[h, j], q_send.at[h, j], q_recv.at[h, j], at.dev(dzl=dzl, dy=dy))

    kv = []
    for h in range(2):
        each(1, 8, lambda j: q_copy(h, j).start())
        kv.append([])
        for d in (1, 3, 2):
            for i, (ref, buf) in enumerate(((k_ref, kbuf), (v_ref, vbuf))):
                copy = remote(ref.at[:, heads[h]], buf.at[h, d], kv_send.at[i, h, d], kv_recv.at[i, h, d], at.dev(dx=d))
                copy.start()
                kv[h].append(copy)
    meta_copy = remote(meta, other, m_send, m_recv, at.dev(dzl=1))
    meta_copy.start()
    weights, swap = [], []
    for i, (src, dst) in enumerate(((eg_ref, wg), (eu_ref, wu), (ed_ref, wd))):
        weights.append(load(8 + i, src.at[0], dst.at[0:352]))
        copy = remote(src.at[0], dst.at[352:704], w_send.at[i], w_recv.at[i], at.dev(dk=1))
        copy.start()
        swap.append(copy)

    key_row = lax.broadcasted_iota(jnp.int32, (512, 128), 0)
    lanes = lax.broadcasted_iota(jnp.int32, (512, 128), 1)
    from_x = lax.rem(at.x - lax.div(key_row, 128) + 4, 4)
    key_spot = (zl * 16 + from_x * 4 + at.y) * 128 + lax.rem(key_row, 128) - lanes

    def back(h, j):
        device = at.dev(dzl=lax.div(j, 4), dy=4 - lax.rem(j, 4))
        return remote(obuf.at[h, j], rbuf.at[h, j], o_send.at[h, j], o_recv.at[h, j], device)

    for h in range(2):
        for copy in own_kv[h]:
            copy.wait()
        for copy in kv[h]:
            copy.wait_recv()

        def one_block(j):
            @pl.when(j > 0)
            def _():
                q_copy(h, j).wait_recv()

            q_zl = lax.rem(zl + lax.div(j, 4), 2)
            q_y = lax.rem(at.y + 4 - lax.rem(j, 4), 4)
            allowed = key_spot <= (q_zl * 16 + at.x * 4 + q_y) * 128
            s = nt_dot(kbuf[h].reshape(512, HEAD_DIM), qbuf[h, j])
            s = jnp.where(allowed, s * (math.log2(math.e) / math.sqrt(HEAD_DIM)), NEGATIVE)
            m = jnp.max(s, axis=0, keepdims=True)
            w = jnp.exp2(s - m)
            l = jnp.sum(w, axis=0, keepdims=True)
            o = tn_dot(vbuf[h].reshape(512, HEAD_DIM), w.astype(BF16))
            obuf[h, j, 0:128, :] = o.astype(BF16)
            stats = pieces(m) + pieces(l) + [m, l]
            obuf[h, j, 128:144, :] = jnp.concatenate(stats + stats, axis=0).astype(BF16)

            @pl.when(j > 0)
            def _():
                back(h, j).start()

        each(0, 8, one_block)

    for h in range(2):
        rbuf[h, 0] = obuf[h, 0]
        for j in range(1, 8):
            back(h, j).wait_recv()
        stats = [rbuf[h, j, 128:144, :].astype(F32) for j in range(8)]
        tops = [st[0:1] + st[1:2] + st[2:3] for st in stats]
        top = tops[0]
        for j in range(1, 8):
            top = jnp.maximum(top, tops[j])
        total = jnp.zeros((HEAD_DIM, 128), F32)
        denom = jnp.zeros((1, 128), F32)
        for j in range(8):
            w = jnp.exp2(tops[j] - top)
            denom += w * (stats[j][3:4] + stats[j][4:5] + stats[j][5:6])
            total += w * rbuf[h, j, 0:128, :].astype(F32)
        att[h * HEAD_DIM:(h + 1) * HEAD_DIM, :] = (total / denom).astype(BF16)

    load_w.wait()
    load_r.wait()
    swaps, sums = [], []
    for n in range(CHUNKS):
        part = tn_dot(att[...], ow[:, chunk[n]]).astype(BF16)
        for b in range(8):
            pbuf[b % 2, b // 2, :, chunk[n]] = part[16 * b:16 * b + 16]
        copy = remote(pbuf.at[1 - k, :, :, chunk[n]], sbuf.at[:, :, chunk[n]], c_send.at[n], c_recv.at[n], at.dev(dk=1))
        copy.start()
        swaps.append(copy)
    for n in range(CHUNKS):
        swaps[n].wait_recv()
        tbuf[:, :, chunk[n]] = (
            pbuf[k, :, :, chunk[n]].astype(F32) + sbuf[:, :, chunk[n]].astype(F32)
        ).astype(BF16)
        for d in (2, 1, 3):
            copy = remote(
                tbuf.at[lax.rem(zh + d, 4), :, chunk[n]], zbuf.at[d - 1, :, chunk[n]],
                z_send.at[n, d], z_recv.at[n, d], at.dev(dzh=d),
            )
            copy.start()
            sums.append(copy)
    meta_copy.wait_recv()
    selection(at, jnp.where(even, meta[...], other[...]), text_map, back_map, image_map)
    power = jnp.zeros((16, 1), F32)
    for n in range(CHUNKS):
        for copy in sums[3 * n:3 * n + 3]:
            copy.wait_recv()
        total = pbuf[k, zh, :, chunk[n]].astype(F32) + sbuf[zh, :, chunk[n]].astype(F32)
        for d in range(3):
            total += zbuf[d, :, chunk[n]].astype(F32)
        total += res[:, chunk[n]].astype(F32)
        state[:, chunk[n]] = total
        power += jnp.sum(total * total, axis=-1, keepdims=True)
    scale = lax.rsqrt(power / WIDTH + EPSILON)
    for n in range(CHUNKS):
        normed[:, chunk[n]] = (state[:, chunk[n]] * scale * gain_ref[:, chunk[n]]).astype(BF16)

    def gather(dz, n):
        return remote(
            normed.at[:, chunk[n]], rows.at[zh, k, :, chunk[n]],
            g_send.at[dz, n], g_recv.at[dz, k, n], at.column(dz, zl),
        )

    def gathered(dz, core, n):
        origin = lax.div(lax.rem(z - dz + 8, 8), 2)
        part = rows.at[origin, core, :, chunk[n]]
        return remote(part, part, g_send.at[dz, n], g_recv.at[dz, core, n], at.column(dz, zl))

    for n in range(CHUNKS):
        @pl.when(odd)
        def _():
            gather(0, n).start()

        for dz in (4, 3, 5, 2, 6, 1, 7):
            gather(dz, n).start()

    @pl.when(even)
    def _():
        rows[zh, k] = normed[...]

    own = wi.at[at.e]
    image_copies = [remote(own, own, i_send.at[0], i_recv.at[0], at.dev(dk=1))]
    image_copies += [remote(own, own, i_send.at[d], i_recv.at[d], at.dev(dzh=d)) for d in (1, 2, 3)]
    for copy in image_copies:
        copy.start()

    def text_copy(t, n):
        return remote(tsend.at[t, :, chunk[n]], xt.at[t, :, chunk[n]], d_send.at[t, n], d_recv.at[t, n], at.plane(t))

    def first_hop(d, n):
        src = xi.at[0, 0, :, chunk[n]]
        if n % 2 == 0:
            return remote(src, xi.at[0, d, :, chunk[n]], x1_send.at[d, n], x1_recv.at[d, n], at.dev(dx=d))
        return remote(src, xi.at[d, 0, :, chunk[n]], x1_send.at[d, n], x1_recv.at[d, n], at.dev(dy=d))

    def second_hop(d, n):
        if n % 2 == 0:
            src, dst, device = xi.at[0, :, :, chunk[n]], xi.at[d, :, :, chunk[n]], at.dev(dy=d)
        else:
            src, dst, device = xi.at[:, 0, :, chunk[n]], xi.at[:, d, :, chunk[n]], at.dev(dx=d)
        return remote(src, dst, x2_send.at[d, n], x2_recv.at[d, n], device)

    def dispatch(n):
        for i in range(1, 4):
            for core in range(2):
                gathered(p + 2 * i, core, n).wait_recv()

        @pl.when(even)
        def _():
            gathered(0, 1 - k, n).wait_recv()

        @pl.when(odd)
        def _():
            for core in range(2):
                gathered(1, core, n).wait_recv()

        part = rows[:, :, :, chunk[n]].reshape(128, CHUNK)
        xi[0, 0, :, chunk[n]] = jnp.dot(image_map[...], part, preferred_element_type=F32).astype(BF16)
        for d in (1, 3, 2):
            first_hop(d, n).start()
        picked = jnp.dot(text_map[...], part, preferred_element_type=F32).astype(BF16).reshape(16, 16, CHUNK)
        tsend[:, :, chunk[n]] = picked
        xt[0, :, chunk[n]] = picked[0]
        each(1, 16, lambda t: text_copy(t, n).start())

    def forward(n):
        for d in (1, 3, 2):
            first_hop(d, n).wait_recv()
        for d in (1, 3, 2):
            second_hop(d, n).start()

    for n in range(CHUNKS):
        dispatch(n)
        if n > 0:
            forward(n - 1)
    forward(CHUNKS - 1)

    for copy in weights[:2]:
        copy.wait()
    for copy in swap[:2]:
        copy.wait_recv()
    for n in range(CHUNKS):
        each(1, 16, lambda t: text_copy(t, n).wait_recv())
        part = xt[:, :, chunk[n]].reshape(256, CHUNK)
        for i, w in enumerate((wg, wu)):
            term = nt_dot(part, w[:, chunk[n]])
            if n == 0:
                acc[i] = term
            else:
                acc[i] += term
    text_act = active(acc[0], acc[1])
    weights[2].wait()
    swap[2].wait_recv()

    def text_back(t, n):
        return remote(
            ysend.at[t, :, chunk[n]], ys.at[t, :, chunk[n]], t_send.at[t, n], t_recv.at[t, n], at.plane(t, True)
        )

    for n in range(CHUNKS):
        result = jnp.dot(text_act, wd[:, chunk[n]], preferred_element_type=F32).astype(BF16).reshape(16, 16, CHUNK)
        ysend[:, :, chunk[n]] = result
        ys[0, :, chunk[n]] = result[0]
        each(1, 16, lambda t: text_back(t, n).start())

    def image_arrival(d):
        part = wi.at[2 * lax.rem(zh + 4 - d, 4) + k]
        return remote(part, part, i_send.at[d], i_recv.at[d], at.dev(dzh=d))

    def image_pass(d):
        part = wi.at[2 * lax.rem(zh + 4 - d, 4) + k]
        return remote(part, part, f_send.at[d], f_recv.at[d], at.dev(dk=1))

    def image_passed(d):
        part = wi.at[2 * lax.rem(zh + 4 - d, 4) + 1 - k]
        return remote(part, part, f_send.at[d], f_recv.at[d], at.dev(dk=1))

    for d in (1, 3, 2):
        image_arrival(d).wait_recv()
        image_pass(d).start()
    remote(own, wi.at[2 * zh + 1 - k], i_send.at[0], i_recv.at[0], at.dev(dk=1)).wait_recv()
    for d in (1, 3, 2):
        image_passed(d).wait_recv()
    gate_up = jnp.zeros((256, 352), F32)
    for n in range(CHUNKS):
        for d in (1, 3, 2):
            second_hop(d, n).wait_recv()
        for e in (2 * n, 2 * n + 1):
            part = xi[:, :, :, e * 512:(e + 1) * 512].reshape(256, 512)
            gate_up += nt_dot(part, wi[e, 0:2].reshape(352, 512))
    image_act = active(gate_up[:, 0:176], gate_up[:, 176:352])

    def sum_one(d, n):
        if n % 2 == 0:
            src, device = isend.at[d, :, :, chunk[n]], at.dev(dy=4 - d)
        else:
            src, device = isend.at[:, d, :, chunk[n]], at.dev(dx=4 - d)
        return remote(src, ir1.at[d - 1, :, :, chunk[n]], y1_send.at[d, n], y1_recv.at[d, n], device)

    def sum_two(d, n):
        device = at.dev(dx=4 - d) if n % 2 == 0 else at.dev(dy=4 - d)
        return remote(is2.at[d, :, chunk[n]], ir2.at[d - 1, :, chunk[n]], y2_send.at[d, n], y2_recv.at[d, n], device)

    def image_down(n):
        result = jnp.concatenate(
            [jnp.dot(image_act, wi[e, 2], preferred_element_type=F32) for e in (2 * n, 2 * n + 1)], axis=1
        )
        isend[:, :, :, chunk[n]] = result.astype(BF16).reshape(4, 4, 16, CHUNK)
        for d in (1, 3, 2):
            sum_one(d, n).start()

    def image_turn(n):
        total = (isend[0, :, :, chunk[n]] if n % 2 == 0 else isend[:, 0, :, chunk[n]]).astype(F32)
        for d in (1, 3, 2):
            sum_one(d, n).wait_recv()
            total += ir1[d - 1, :, :, chunk[n]].astype(F32)
        is2[:, :, chunk[n]] = total.astype(BF16)
        for d in (1, 3, 2):
            sum_two(d, n).start()

    def to_owner(i, core, n):
        dz = p + 2 * i
        target = lax.div(lax.rem(z + dz, 8), 2) * 2 + core
        return remote(
            zsend.at[target, :, chunk[n]], zrecv.at[dz, :, chunk[n]],
            e_send.at[i, core, n], e_recv.at[dz, n], at.column(dz, core),
        )

    def from_column(dz, n):
        part = zrecv.at[dz, :, chunk[n]]
        return remote(part, part, e_send.at[0, 0, n], e_recv.at[dz, n], at.column(dz, k))

    def combine(n):
        each(1, 16, lambda t: text_back(t, n).wait_recv())
        image_total = is2[0, :, chunk[n]].astype(F32)
        for d in (1, 3, 2):
            sum_two(d, n).wait_recv()
            image_total += ir2[d - 1, :, chunk[n]].astype(F32)
        total = tn_dot(back_map[...], ys[:, :, chunk[n]].reshape(256, CHUNK))
        total += tn_dot(image_map[...], image_total.astype(BF16))
        total = total.reshape(8, 16, CHUNK)
        zsend[:, :, chunk[n]] = total.astype(BF16)
        for i in (2, 1, 3):
            for core in range(2):
                to_owner(i, core, n).start()

        @pl.when(odd)
        def _():
            for core in range(2):
                to_owner(0, core, n).start()

        @pl.when(even)
        def _():
            to_owner(0, 1 - k, n).start()
            zown[:, chunk[n]] = zsend[at.e, :, chunk[n]].astype(F32)

        @pl.when(odd)
        def _():
            zown[:, chunk[n]] = jnp.zeros((16, CHUNK), F32)

    def finish(n):
        total = state[:, chunk[n]] + zown[:, chunk[n]]
        for dz in range(1, 8):
            from_column(dz, n).wait_recv()
            total += zrecv[dz, :, chunk[n]].astype(F32)
        out_ref[:, chunk[n]] = total.astype(BF16)

        @pl.when(odd)
        def _():
            from_column(0, n).wait_recv()
            out_ref[:, chunk[n]] = (total + zrecv[0, :, chunk[n]].astype(F32)).astype(BF16)

    for n in range(CHUNKS):
        image_down(n)
        if n > 0:
            image_turn(n - 1)
    image_turn(CHUNKS - 1)
    for n in range(CHUNKS):
        combine(n)
        if n > 0:
            finish(n - 1)
    finish(CHUNKS - 1)

    meta_copy.wait_send()
    for copy in kv[0] + kv[1] + swap + swaps + sums + image_copies:
        copy.wait_send()
    for h in range(2):
        def sent_a(j):
            q_copy(h, j).wait_send()
            back(h, j).wait_send()

        each(1, 8, sent_a)
    for d in (1, 2, 3):
        image_pass(d).wait_send()
    for n in range(CHUNKS):
        def sent_b(t):
            text_copy(t, n).wait_send()
            text_back(t, n).wait_send()

        each(1, 16, sent_b)
        for dz in range(1, 8):
            gather(dz, n).wait_send()
        for d in (1, 2, 3):
            first_hop(d, n).wait_send()
            second_hop(d, n).wait_send()
            sum_one(d, n).wait_send()
            sum_two(d, n).wait_send()
            for core in range(2):
                to_owner(d, core, n).wait_send()

        @pl.when(odd)
        def _():
            gather(0, n).wait_send()
            for core in range(2):
                to_owner(0, core, n).wait_send()

        @pl.when(even)
        def _():
            to_owner(0, 1 - k, n).wait_send()


def body(
    query, keys, values, resid, flags, routes, gates, out_weight, norm_gain,
    img_gate, img_up, img_down, exp_gate, exp_up, exp_down,
):
    vmem, hbm = pl.BlockSpec(memory_space=pltpu.VMEM), pl.BlockSpec(memory_space=pl.ANY)
    dma = pltpu.SemaphoreType.DMA

    def buf(*shape, dtype=BF16):
        return pltpu.VMEM(shape, dtype)

    def pair(*shape):
        return [dma(shape), dma(shape)]

    return pl.pallas_call(
        layer_kernel,
        name="layer",
        out_shape=jax.ShapeDtypeStruct((16, WIDTH), BF16),
        in_specs=[hbm] * 4 + [vmem] * 3 + [hbm, vmem] + [vmem] * 3 + [hbm] * 3,
        out_specs=vmem,
        scratch_shapes=[
            buf(2, 4, 128, 128), buf(2, 4, 128, 128), buf(2, 8, 128, 128), buf(2, 8, 144, 128), buf(2, 8, 144, 128),
            buf(256, WIDTH), buf(16, WIDTH), buf(256, 128),
            buf(2, 4, 16, WIDTH), buf(4, 16, WIDTH), buf(4, 16, WIDTH), buf(3, 16, WIDTH),
            buf(16, WIDTH, dtype=F32), buf(16, WIDTH),
            buf(704, WIDTH), buf(704, WIDTH), buf(704, WIDTH), buf(8, 3, 176, 512),
            buf(16, 128, dtype=F32), buf(16, 128, dtype=F32), buf(256, 128), buf(256, 128), buf(16, 128),
            buf(4, 2, 16, WIDTH), buf(16, 16, WIDTH), buf(16, 16, WIDTH), buf(4, 4, 16, WIDTH),
            buf(2, 256, 704, dtype=F32),
            buf(16, 16, WIDTH), buf(16, 16, WIDTH), buf(4, 4, 16, WIDTH), buf(3, 4, 16, WIDTH),
            buf(4, 16, WIDTH), buf(3, 16, WIDTH), buf(8, 16, WIDTH), buf(8, 16, WIDTH), buf(16, WIDTH, dtype=F32),
            *pair(2, 2, 4), *pair(2, 8), *pair(2, 8), *pair(CHUNKS), *pair(CHUNKS, 4), dma((11,)),
            *pair(3), dma, dma, dma((8, CHUNKS)), dma((8, 2, CHUNKS)), *pair(16, CHUNKS),
            *pair(4, CHUNKS), *pair(4, CHUNKS), *pair(4), *pair(4), *pair(16, CHUNKS),
            *pair(4, CHUNKS), *pair(4, CHUNKS), dma((4, 2, CHUNKS)), dma((8, CHUNKS)),
        ],
        compiler_params=pltpu.CompilerParams(
            collective_id=1, has_side_effects=True, vmem_limit_bytes=60 << 20
        ),
    )(
        query, keys, values, resid, flags.reshape(1, -1), routes.T, gates.T, out_weight, norm_gain.reshape(1, WIDTH),
        img_gate.T, img_up.T, img_down.T,
        exp_gate.transpose(0, 2, 1), exp_up.transpose(0, 2, 1), exp_down,
    )


def solution(mesh):
    return jax.shard_map(
        body,
        mesh=mesh,
        in_specs=(
            P("ctx", "exp"),
            P("ctx", "exp"),
            P("ctx", "exp"),
            P("ctx", None),
            P("ctx"),
            P("ctx", None),
            P("ctx", None),
            P("exp", None),
            P(),
            P("exp", "ctx"),
            P("exp", "ctx"),
            P("exp", "ctx"),
            P(("ctx", "exp"), None, None),
            P(("ctx", "exp"), None, None),
            P(("ctx", "exp"), None, None),
        ),
        out_specs=P(("ctx", "exp"), None),
        check_vma=False,
    )
```

```python
import math

import jax
import jax.numpy as jnp
from jax import lax
from jax.experimental import pallas as pl
from jax.experimental.pallas import tpu as pltpu
from jax.sharding import PartitionSpec as P

MESH = pl.DeviceIdType.MESH
HEAD_DIM = 128
NEGATIVE = -1e30
EPSILON = 1e-05
WIDTH = 4096
CHUNK = 1024
CHUNKS = WIDTH // CHUNK
SCALE = WIDTH
WIDE = WIDTH + 128
BF16 = jnp.bfloat16
F32 = jnp.float32


class Place:
    def __init__(self):
        c, e = lax.axis_index("ctx"), lax.axis_index("exp")
        self.e = e
        self.zl, self.x, self.y = lax.div(c, 16), lax.rem(lax.div(c, 4), 4), lax.rem(c, 4)
        self.zh, self.k = lax.div(e, 2), lax.rem(e, 2)
        self.z = self.zh * 2 + self.zl

    def dev(self, dx=0, dy=0, dzl=0, dzh=0, dk=0):
        x, y = lax.rem(self.x + dx + 4, 4), lax.rem(self.y + dy + 4, 4)
        zl, zh, k = lax.rem(self.zl + dzl, 2), lax.rem(self.zh + dzh + 4, 4), lax.rem(self.k + dk, 2)
        return (zl * 16 + x * 4 + y, zh * 2 + k)

    def column(self, dz, core):
        z = lax.rem(self.z + dz + 8, 8)
        return (lax.rem(z, 2) * 16 + self.x * 4 + self.y, lax.div(z, 2) * 2 + core)

    def plane(self, t, back=False):
        dx, dy = lax.div(t, 4), lax.rem(t, 4)
        return self.dev(dx=4 - dx, dy=4 - dy) if back else self.dev(dx=dx, dy=dy)


def remote(src, dst, send, recv, device):
    return pltpu.make_async_remote_copy(
        src_ref=src, dst_ref=dst, send_sem=send, recv_sem=recv, device_id=device, device_id_type=MESH
    )


def nt_dot(a, b):
    return lax.dot_general(a, b, (((1,), (1,)), ((), ())), preferred_element_type=F32)


def tn_dot(a, b):
    return lax.dot_general(a, b, (((0,), (0,)), ((), ())), preferred_element_type=F32)


def pieces(value):
    first = value.astype(BF16).astype(F32)
    second = (value - first).astype(BF16).astype(F32)
    return [first, second, value - first - second]


def active(gate, up):
    return (gate / (1.0 + jnp.exp(-gate)) * up).astype(BF16)


def each(low, high, step):
    def go(t, carried):
        step(t)
        return carried

    lax.fori_loop(low, high, go, 0)


def selection(at, meta, text_map, back_map, image_map):
    lane = lax.broadcasted_iota(jnp.int32, (16, 128), 1)
    spot = lax.broadcasted_iota(jnp.int32, (16, 128), 0)
    to_x = lax.rem(at.x + lax.div(spot, 4), 4)
    to_y = lax.rem(at.y + lax.rem(spot, 4), 4)
    expert = (2 * (at.zl * 16 + to_x * 4 + to_y) + lax.div(at.zh, 2)).astype(F32)
    chosen = jnp.zeros((16, 128), F32)
    gate = jnp.zeros((16, 128), F32)
    for j in range(6):
        hit = jnp.where(meta[j:j + 1, :] == expert, 1.0, 0.0)
        chosen += hit
        gate += hit * meta[6 + j:7 + j, :]
    image = jnp.broadcast_to(meta[12:13, :], (16, 128))
    chosen = jnp.where(image == 0.0, chosen, 0.0)
    gate = jnp.where(image == 0.0, gate, 0.0)
    row = lax.broadcasted_iota(jnp.int32, (128, 128), 0)
    col = lax.broadcasted_iota(jnp.int32, (128, 128), 1)
    earlier = jnp.where((lax.div(row, 16) == lax.div(col, 16)) & (row < col), 1.0, 0.0).astype(BF16)
    rank = jnp.dot(jnp.concatenate([chosen, image], axis=0).astype(BF16), earlier, preferred_element_type=F32)
    sub = lax.div(lane, 16)
    text_slot = jnp.where(chosen > 0.0, (2 * sub).astype(F32) + rank[0:16], -1.0)
    mine = (image > 0.0) & (lax.div(sub, 2) == at.zh)
    image_slot = jnp.where(mine, (8 * (sub - 2 * at.zh)).astype(F32) + rank[16:32], -1.0)
    slot = spot.astype(F32)
    image_map[...] = jnp.where(image_slot == slot, 1.0, 0.0).astype(BF16)
    for t in range(16):
        match = text_slot[t:t + 1, :] == slot
        text_map[16 * t:16 * t + 16, :] = jnp.where(match, 1.0, 0.0).astype(BF16)
        back_map[16 * t:16 * t + 16, :] = jnp.where(match, gate[t:t + 1, :], 0.0).astype(BF16)


def layer_kernel(
    q_ref, k_ref, v_ref, resid_ref, flags_ref, routes_ref, gates_ref, ow_ref, gain_ref,
    ig_ref, iu_ref, id_ref, eg_ref, eu_ref, ed_ref,
    out_ref,
    kbuf, vbuf, qbuf, obuf, rbuf, ow, res, att, pbuf, sbuf, tbuf, zbuf, state, normed,
    wg, wu, wd, wi, meta, other, text_map, back_map, image_map, rows, tsend, xt, xi, acc,
    ysend, ys, isend, ir1, is2, ir2, zsend, zrecv, zown,
    kv_send, kv_recv, q_send, q_recv, o_send, o_recv, c_send, c_recv, z_send, z_recv, local_sem,
    w_send, w_recv, m_send, m_recv, p_send, p_recv, g_send, g_recv, d_send, d_recv, x1_send, x1_recv, x2_send, x2_recv,
    i_send, i_recv, f_send, f_recv, h_send, h_recv, t_send, t_recv, y1_send, y1_recv, y2_send, y2_recv, e_send, e_recv,
):
    at = Place()
    z, k, zh, zl = at.z, at.k, at.zh, at.zl
    p = lax.rem(zl + k, 2)
    even, odd = p == 0, p == 1
    side_step = 1 - 2 * k
    chunk = [pl.ds(n * CHUNK, CHUNK) for n in range(CHUNKS)]
    size = [CHUNK] * (CHUNKS - 1) + [CHUNK + WIDE - WIDTH]
    wide = [pl.ds(n * CHUNK, size[n]) for n in range(CHUNKS)]
    heads = [pl.ds(h * HEAD_DIM, HEAD_DIM) for h in range(2)]

    def load(i, src, dst):
        copy = pltpu.make_async_copy(src, dst, local_sem.at[i])
        copy.start()
        return copy

    own_kv = []
    for h in range(2):
        own_kv.append([
            load(3 * h, q_ref.at[:, heads[h]], qbuf.at[h, 0]),
            load(3 * h + 1, k_ref.at[:, heads[h]], kbuf.at[h, 0]),
            load(3 * h + 2, v_ref.at[:, heads[h]], vbuf.at[h, 0]),
        ])
    own_rows = pl.ds(pl.multiple_of(at.e * 16, 16), 16)
    load_r = load(6, resid_ref.at[own_rows], res)
    load_w = load(7, ow_ref, ow)
    barrier = pltpu.get_barrier_semaphore()
    partners = [at.plane(t) for t in range(1, 16)]
    partners += [at.column(dz, lax.rem(k + dk, 2)) for dz in range(8) for dk in range(2) if (dz, dk) != (0, 0)]
    partners += [at.dev(dzl=1, dy=d) for d in (1, 2, 3)]
    for device in partners:
        pl.semaphore_signal(barrier, inc=1, device_id=device, device_id_type=MESH)
    meta[0:6, :] = routes_ref[...].astype(F32)
    meta[6:12, :] = gates_ref[...].astype(F32)
    meta[12:16, :] = jnp.broadcast_to(flags_ref[...].astype(F32), (4, 128))
    pad = jnp.zeros((4, 512), BF16)
    for i, ref in enumerate((ig_ref, iu_ref, id_ref)):
        wi[at.e, i] = jnp.concatenate([ref[...], pad], axis=0)
    pl.semaphore_wait(barrier, len(partners))

    def q_copy(h, j):
        dy, dzl = lax.rem(j, 4), lax.div(j, 4)
        return remote(q_ref.at[:, heads[h]], qbuf.at[h, j], q_send.at[h, j], q_recv.at[h, j], at.dev(dzl=dzl, dy=dy))

    kv = []
    for h in range(2):
        each(1, 8, lambda j: q_copy(h, j).start())
        kv.append([])
        for d in (1, 3, 2):
            for i, (ref, buf) in enumerate(((k_ref, kbuf), (v_ref, vbuf))):
                copy = remote(ref.at[:, heads[h]], buf.at[h, d], kv_send.at[i, h, d], kv_recv.at[i, h, d], at.dev(dx=d))
                copy.start()
                kv[h].append(copy)
    meta_copy = remote(meta, other, m_send, m_recv, at.dev(dzl=1))
    meta_copy.start()
    weights, swap = [], []
    for i, (src, dst) in enumerate(((eg_ref, wg), (eu_ref, wu), (ed_ref, wd))):
        weights.append(load(8 + i, src.at[0], dst.at[0:352]))
        copy = remote(src.at[0], dst.at[352:704], w_send.at[i], w_recv.at[i], at.dev(dk=1))
        copy.start()
        swap.append(copy)

    key_row = lax.broadcasted_iota(jnp.int32, (512, 128), 0)
    lanes = lax.broadcasted_iota(jnp.int32, (512, 128), 1)
    from_x = lax.rem(at.x - lax.div(key_row, 128) + 4, 4)
    key_spot = (zl * 16 + from_x * 4 + at.y) * 128 + lax.rem(key_row, 128) - lanes

    def back(h, j):
        device = at.dev(dzl=lax.div(j, 4), dy=4 - lax.rem(j, 4))
        return remote(obuf.at[h, j], rbuf.at[h, j], o_send.at[h, j], o_recv.at[h, j], device)

    for h in range(2):
        for copy in own_kv[h]:
            copy.wait()
        for copy in kv[h]:
            copy.wait_recv()

        def one_block(j):
            @pl.when(j > 0)
            def _():
                q_copy(h, j).wait_recv()

            q_zl = lax.rem(zl + lax.div(j, 4), 2)
            q_y = lax.rem(at.y + 4 - lax.rem(j, 4), 4)
            allowed = key_spot <= (q_zl * 16 + at.x * 4 + q_y) * 128
            s = nt_dot(kbuf[h].reshape(512, HEAD_DIM), qbuf[h, j])
            s = jnp.where(allowed, s * (math.log2(math.e) / math.sqrt(HEAD_DIM)), NEGATIVE)
            m = jnp.max(s, axis=0, keepdims=True)
            w = jnp.exp2(s - m)
            l = jnp.sum(w, axis=0, keepdims=True)
            o = tn_dot(vbuf[h].reshape(512, HEAD_DIM), w.astype(BF16))
            obuf[h, j, 0:128, :] = o.astype(BF16)
            stats = pieces(m) + pieces(l) + [m, l]
            obuf[h, j, 128:144, :] = jnp.concatenate(stats + stats, axis=0).astype(BF16)

            @pl.when(j > 0)
            def _():
                back(h, j).start()

        each(0, 8, one_block)

    for h in range(2):
        rbuf[h, 0] = obuf[h, 0]
        for j in range(1, 8):
            back(h, j).wait_recv()
        stats = [rbuf[h, j, 128:144, :].astype(F32) for j in range(8)]
        tops = [st[0:1] + st[1:2] + st[2:3] for st in stats]
        top = tops[0]
        for j in range(1, 8):
            top = jnp.maximum(top, tops[j])
        total = jnp.zeros((HEAD_DIM, 128), F32)
        denom = jnp.zeros((1, 128), F32)
        for j in range(8):
            w = jnp.exp2(tops[j] - top)
            denom += w * (stats[j][3:4] + stats[j][4:5] + stats[j][5:6])
            total += w * rbuf[h, j, 0:128, :].astype(F32)
        att[h * HEAD_DIM:(h + 1) * HEAD_DIM, :] = (total / denom).astype(BF16)

    load_w.wait()
    load_r.wait()
    swaps, sums = [], []
    for n in range(CHUNKS):
        part = tn_dot(att[...], ow[:, chunk[n]]).astype(BF16)
        for b in range(8):
            pbuf[b % 2, b // 2, :, chunk[n]] = part[16 * b:16 * b + 16]
        copy = remote(pbuf.at[1 - k, :, :, chunk[n]], sbuf.at[:, :, chunk[n]], c_send.at[n], c_recv.at[n], at.dev(dk=1))
        copy.start()
        swaps.append(copy)
    for n in range(CHUNKS):
        swaps[n].wait_recv()
        tbuf[:, :, chunk[n]] = (
            pbuf[k, :, :, chunk[n]].astype(F32) + sbuf[:, :, chunk[n]].astype(F32)
        ).astype(BF16)
        for d in (2, 1, 3):
            copy = remote(
                tbuf.at[lax.rem(zh + d, 4), :, chunk[n]], zbuf.at[d - 1, :, chunk[n]],
                z_send.at[n, d], z_recv.at[n, d], at.dev(dzh=d),
            )
            copy.start()
            sums.append(copy)
    meta_copy.wait_recv()
    selection(at, jnp.where(even, meta[...], other[...]), text_map, back_map, image_map)
    powers = []

    def norm_step(n):
        for copy in sums[3 * n:3 * n + 3]:
            copy.wait_recv()
        total = pbuf[k, zh, :, chunk[n]].astype(F32) + sbuf[zh, :, chunk[n]].astype(F32)
        for d in range(3):
            total += zbuf[d, :, chunk[n]].astype(F32)
        total += res[:, chunk[n]].astype(F32)
        state[:, chunk[n]] = total
        powers.append(jnp.sum(total * total, axis=-1, keepdims=True))
        normed[:, chunk[n]] = (total * gain_ref[:, chunk[n]]).astype(BF16)
        if n == CHUNKS - 1:
            scale = jnp.broadcast_to(lax.rsqrt(sum(powers) / WIDTH + EPSILON), (16, 64))
            high = scale.astype(BF16)
            low = (scale - high.astype(F32)).astype(BF16)
            normed[:, SCALE:WIDE] = jnp.concatenate([high, low], axis=1)

        @pl.when(odd)
        def _():
            pair_copy(n).start()

        @pl.when(even)
        def _():
            rows[zh, k, :, wide[n]] = normed[:, wide[n]]
            pair_arrival(n).wait_recv()
            ring_copy(0, 0, n).start()
            ring_copy(1, 0, n).start()

    def pair_copy(n):
        return remote(
            normed.at[:, wide[n]], rows.at[zh, k, :, wide[n]], p_send.at[n], p_recv.at[n], at.dev(dk=1)
        )

    def pair_arrival(n):
        part = rows.at[zh, 1 - k, :, wide[n]]
        return remote(part, part, p_send.at[n], p_recv.at[n], at.dev(dk=1))

    def ring_part(side, steps, n):
        step = steps * side_step
        origin = lax.rem(z - step + 16, 8) if side == 0 else lax.rem(z + step + 16, 8)
        return rows.at[lax.div(origin, 2), :, :, wide[n]]

    def ring_remote(side, i, n, part):
        device = at.column(side_step if side == 0 else -side_step, k)
        return remote(part, part, g_send.at[side, i, n], g_recv.at[side, i, n], device)

    def ring_copy(side, i, n):
        return ring_remote(side, i, n, ring_part(side, 2 * i + p, n))

    def ring_arrival(side, i, n):
        return ring_remote(side, i, n, ring_part(side, 2 * i + 2 - p, n))

    def ring_one(n):
        for side in range(2):
            ring_arrival(side, 0, n).wait_recv()

            @pl.when(even)
            def _():
                ring_copy(side, 1, n).start()

            @pl.when(odd)
            def _():
                ring_copy(side, 0, n).start()

    def ring_two(n):
        ring_arrival(0, 1, n).wait_recv()

        @pl.when(odd)
        def _():
            ring_copy(0, 1, n).start()
            ring_arrival(1, 1, n).wait_recv()

    own = wi.at[at.e]
    image_copies = [remote(own, own, i_send.at[0], i_recv.at[0], at.dev(dk=1))]
    image_copies += [remote(own, own, i_send.at[d], i_recv.at[d], at.dev(dzh=d)) for d in (1, 3)]

    def image_piece(d, core):
        return wi.at[2 * lax.rem(zh + 4 - d, 4) + core]

    def image_arrival(d):
        part = image_piece(d, k)
        return remote(part, part, i_send.at[d], i_recv.at[d], at.dev(dzh=d))

    def image_half(d):
        part = image_piece(d, k).at[:, :, 0:256] if d == 1 else image_piece(d, k).at[:, :, 256:512]
        return remote(part, part, h_send.at[d], h_recv.at[d], at.dev(dzh=d))

    def image_half_arrival(d):
        part = image_piece(2, k).at[:, :, 0:256] if d == 1 else image_piece(2, k).at[:, :, 256:512]
        return remote(part, part, h_send.at[d], h_recv.at[d], at.dev(dzh=d))

    def image_pass(d):
        part = image_piece(d, k)
        return remote(part, part, f_send.at[d], f_recv.at[d], at.dev(dk=1))

    def image_passed(d):
        part = image_piece(d, 1 - k)
        return remote(part, part, f_send.at[d], f_recv.at[d], at.dev(dk=1))

    def text_copy(t, n):
        return remote(tsend.at[t, :, wide[n]], xt.at[t, :, wide[n]], d_send.at[t, n], d_recv.at[t, n], at.plane(t))

    def first_hop(d, n):
        src = xi.at[0, 0, :, wide[n]]
        if n % 2 == 0:
            return remote(src, xi.at[0, d, :, wide[n]], x1_send.at[d, n], x1_recv.at[d, n], at.dev(dx=d))
        return remote(src, xi.at[d, 0, :, wide[n]], x1_send.at[d, n], x1_recv.at[d, n], at.dev(dy=d))

    def second_hop(d, n):
        if n % 2 == 0:
            src, dst, device = xi.at[0, :, :, wide[n]], xi.at[d, :, :, wide[n]], at.dev(dy=d)
        else:
            src, dst, device = xi.at[:, 0, :, wide[n]], xi.at[:, d, :, wide[n]], at.dev(dx=d)
        return remote(src, dst, x2_send.at[d, n], x2_recv.at[d, n], device)

    def dispatch(n):
        part = rows[:, :, :, wide[n]].reshape(128, size[n])
        xi[0, 0, :, wide[n]] = jnp.dot(image_map[...], part, preferred_element_type=F32).astype(BF16)
        for d in (1, 3, 2):
            first_hop(d, n).start()
        picked = jnp.dot(text_map[...], part, preferred_element_type=F32).astype(BF16).reshape(16, 16, size[n])
        tsend[:, :, wide[n]] = picked
        xt[0, :, wide[n]] = picked[0]
        each(1, 16, lambda t: text_copy(t, n).start())

    def forward(n):
        for d in (1, 3, 2):
            first_hop(d, n).wait_recv()
        for d in (1, 3, 2):
            second_hop(d, n).start()

    for step in range(CHUNKS + 3):
        if step < CHUNKS:
            norm_step(step)
        if 0 <= step - 1 < CHUNKS:
            ring_one(step - 1)
        if 0 <= step - 2 < CHUNKS:
            ring_two(step - 2)
            if step - 2 == CHUNKS - 1:
                for copy in image_copies:
                    copy.start()
            dispatch(step - 2)
        if 0 <= step - 3 < CHUNKS:
            forward(step - 3)

    for copy in weights[:2]:
        copy.wait()
    for copy in swap[:2]:
        copy.wait_recv()
    for n in range(CHUNKS):
        each(1, 16, lambda t: text_copy(t, n).wait_recv())
        part = xt[:, :, chunk[n]].reshape(256, CHUNK)
        for i, w in enumerate((wg, wu)):
            term = nt_dot(part, w[:, chunk[n]])
            if n == 0:
                acc[i] = term
            else:
                acc[i] += term
        if n == 2:
            for d in (1, 3):
                image_arrival(d).wait_recv()
                image_half(d).start()
                image_pass(d).start()
    text_scale = xt[:, :, SCALE:WIDE].reshape(256, 128).astype(F32)
    text_scale = text_scale[:, 0:1] + text_scale[:, 64:65]
    text_act = active(acc[0] * text_scale, acc[1] * text_scale)
    weights[2].wait()
    swap[2].wait_recv()

    def text_back(t, n):
        return remote(
            ysend.at[t, :, chunk[n]], ys.at[t, :, chunk[n]], t_send.at[t, n], t_recv.at[t, n], at.plane(t, True)
        )

    def text_down(n):
        result = jnp.dot(text_act, wd[:, chunk[n]], preferred_element_type=F32).astype(BF16).reshape(16, 16, CHUNK)
        ysend[:, :, chunk[n]] = result
        ys[0, :, chunk[n]] = result[0]
        each(1, 16, lambda t: text_back(t, n).start())

    text_down(0)
    text_down(1)
    remote(own, wi.at[2 * zh + 1 - k], i_send.at[0], i_recv.at[0], at.dev(dk=1)).wait_recv()
    for d in (1, 3):
        image_half_arrival(d).wait_recv()
    image_pass(2).start()
    for d in (1, 3, 2):
        image_passed(d).wait_recv()
    gate_up = jnp.zeros((256, 352), F32)
    for n in range(CHUNKS):
        for d in (1, 3, 2):
            second_hop(d, n).wait_recv()
        for e in (2 * n, 2 * n + 1):
            part = xi[:, :, :, e * 512:(e + 1) * 512].reshape(256, 512)
            gate_up += nt_dot(part, wi[e, 0:2].reshape(352, 512))
    image_scale = xi[:, :, :, SCALE:WIDE].reshape(256, 128).astype(F32)
    gate_up = gate_up * (image_scale[:, 0:1] + image_scale[:, 64:65])
    image_act = active(gate_up[:, 0:176], gate_up[:, 176:352])

    def sum_one(d, n):
        if n % 2 == 0:
            src, device = isend.at[d, :, :, chunk[n]], at.dev(dy=4 - d)
        else:
            src, device = isend.at[:, d, :, chunk[n]], at.dev(dx=4 - d)
        return remote(src, ir1.at[d - 1, :, :, chunk[n]], y1_send.at[d, n], y1_recv.at[d, n], device)

    def sum_two(d, n):
        device = at.dev(dx=4 - d) if n % 2 == 0 else at.dev(dy=4 - d)
        return remote(is2.at[d, :, chunk[n]], ir2.at[d - 1, :, chunk[n]], y2_send.at[d, n], y2_recv.at[d, n], device)

    def image_down(n):
        result = jnp.concatenate(
            [jnp.dot(image_act, wi[e, 2], preferred_element_type=F32) for e in (2 * n, 2 * n + 1)], axis=1
        )
        isend[:, :, :, chunk[n]] = result.astype(BF16).reshape(4, 4, 16, CHUNK)
        for d in (1, 3, 2):
            sum_one(d, n).start()

    def image_turn(n):
        total = (isend[0, :, :, chunk[n]] if n % 2 == 0 else isend[:, 0, :, chunk[n]]).astype(F32)
        for d in (1, 3, 2):
            sum_one(d, n).wait_recv()
            total += ir1[d - 1, :, :, chunk[n]].astype(F32)
        is2[:, :, chunk[n]] = total.astype(BF16)
        for d in (1, 3, 2):
            sum_two(d, n).start()

    def to_owner(i, core, n):
        dz = p + 2 * i
        target = lax.div(lax.rem(z + dz, 8), 2) * 2 + core
        return remote(
            zsend.at[target, :, chunk[n]], zrecv.at[dz, :, chunk[n]],
            e_send.at[i, core, n], e_recv.at[dz, n], at.column(dz, core),
        )

    def from_column(dz, n):
        part = zrecv.at[dz, :, chunk[n]]
        return remote(part, part, e_send.at[0, 0, n], e_recv.at[dz, n], at.column(dz, k))

    def combine(n):
        each(1, 16, lambda t: text_back(t, n).wait_recv())
        image_total = is2[0, :, chunk[n]].astype(F32)
        for d in (1, 3, 2):
            sum_two(d, n).wait_recv()
            image_total += ir2[d - 1, :, chunk[n]].astype(F32)
        total = tn_dot(back_map[...], ys[:, :, chunk[n]].reshape(256, CHUNK))
        total += tn_dot(image_map[...], image_total.astype(BF16))
        total = total.reshape(8, 16, CHUNK)
        zsend[:, :, chunk[n]] = total.astype(BF16)
        for i in (2, 1, 3):
            for core in range(2):
                to_owner(i, core, n).start()

        @pl.when(odd)
        def _():
            for core in range(2):
                to_owner(0, core, n).start()

        @pl.when(even)
        def _():
            to_owner(0, 1 - k, n).start()
            zown[:, chunk[n]] = zsend[at.e, :, chunk[n]].astype(F32)

        @pl.when(odd)
        def _():
            zown[:, chunk[n]] = jnp.zeros((16, CHUNK), F32)

    def finish(n):
        total = state[:, chunk[n]] + zown[:, chunk[n]]
        for dz in range(1, 8):
            from_column(dz, n).wait_recv()
            total += zrecv[dz, :, chunk[n]].astype(F32)
        out_ref[:, chunk[n]] = total.astype(BF16)

        @pl.when(odd)
        def _():
            from_column(0, n).wait_recv()
            out_ref[:, chunk[n]] = (total + zrecv[0, :, chunk[n]].astype(F32)).astype(BF16)

    image_down(0)
    image_down(1)
    text_down(2)
    image_down(2)
    image_turn(0)
    text_down(3)
    image_down(3)
    for n in range(CHUNKS):
        if n + 1 < CHUNKS:
            image_turn(n + 1)
        combine(n)
        if n > 0:
            finish(n - 1)
    finish(CHUNKS - 1)

    meta_copy.wait_send()
    for copy in kv[0] + kv[1] + swap + swaps + sums + image_copies:
        copy.wait_send()
    for h in range(2):
        def sent_a(j):
            q_copy(h, j).wait_send()
            back(h, j).wait_send()

        each(1, 8, sent_a)
    for d in (1, 2, 3):
        image_pass(d).wait_send()
    for d in (1, 3):
        image_half(d).wait_send()
    for n in range(CHUNKS):
        def sent_b(t):
            text_copy(t, n).wait_send()
            text_back(t, n).wait_send()

        each(1, 16, sent_b)
        for d in (1, 2, 3):
            first_hop(d, n).wait_send()
            second_hop(d, n).wait_send()
            sum_one(d, n).wait_send()
            sum_two(d, n).wait_send()
            for core in range(2):
                to_owner(d, core, n).wait_send()

        for side, i in ((0, 0), (1, 0), (0, 1)):
            ring_copy(side, i, n).wait_send()

        @pl.when(odd)
        def _():
            pair_copy(n).wait_send()
            for core in range(2):
                to_owner(0, core, n).wait_send()

        @pl.when(even)
        def _():
            ring_copy(1, 1, n).wait_send()
            to_owner(0, 1 - k, n).wait_send()


def body(
    query, keys, values, resid, flags, routes, gates, out_weight, norm_gain,
    img_gate, img_up, img_down, exp_gate, exp_up, exp_down,
):
    vmem, hbm = pl.BlockSpec(memory_space=pltpu.VMEM), pl.BlockSpec(memory_space=pl.ANY)
    dma = pltpu.SemaphoreType.DMA

    def buf(*shape, dtype=BF16):
        return pltpu.VMEM(shape, dtype)

    def pair(*shape):
        return [dma(shape), dma(shape)]

    return pl.pallas_call(
        layer_kernel,
        name="layer",
        out_shape=jax.ShapeDtypeStruct((16, WIDTH), BF16),
        in_specs=[hbm] * 4 + [vmem] * 3 + [hbm, vmem] + [vmem] * 3 + [hbm] * 3,
        out_specs=vmem,
        scratch_shapes=[
            buf(2, 4, 128, 128), buf(2, 4, 128, 128), buf(2, 8, 128, 128), buf(2, 8, 144, 128), buf(2, 8, 144, 128),
            buf(256, WIDTH), buf(16, WIDTH), buf(256, 128),
            buf(2, 4, 16, WIDTH), buf(4, 16, WIDTH), buf(4, 16, WIDTH), buf(3, 16, WIDTH),
            buf(16, WIDTH, dtype=F32), buf(16, WIDE),
            buf(704, WIDTH), buf(704, WIDTH), buf(704, WIDTH), buf(8, 3, 176, 512),
            buf(16, 128, dtype=F32), buf(16, 128, dtype=F32), buf(256, 128), buf(256, 128), buf(16, 128),
            buf(4, 2, 16, WIDE), buf(16, 16, WIDE), buf(16, 16, WIDE), buf(4, 4, 16, WIDE),
            buf(2, 256, 704, dtype=F32),
            buf(16, 16, WIDTH), buf(16, 16, WIDTH), buf(4, 4, 16, WIDTH), buf(3, 4, 16, WIDTH),
            buf(4, 16, WIDTH), buf(3, 16, WIDTH), buf(8, 16, WIDTH), buf(8, 16, WIDTH), buf(16, WIDTH, dtype=F32),
            *pair(2, 2, 4), *pair(2, 8), *pair(2, 8), *pair(CHUNKS), *pair(CHUNKS, 4), dma((11,)),
            *pair(3), dma, dma, *pair(CHUNKS), *pair(2, 2, CHUNKS), *pair(16, CHUNKS),
            *pair(4, CHUNKS), *pair(4, CHUNKS), *pair(4), *pair(4), *pair(4), *pair(16, CHUNKS),
            *pair(4, CHUNKS), *pair(4, CHUNKS), dma((4, 2, CHUNKS)), dma((8, CHUNKS)),
        ],
        compiler_params=pltpu.CompilerParams(
            collective_id=1, has_side_effects=True, vmem_limit_bytes=60 << 20
        ),
    )(
        query, keys, values, resid, flags.reshape(1, -1), routes.T, gates.T, out_weight, norm_gain.reshape(1, WIDTH),
        img_gate.T, img_up.T, img_down.T,
        exp_gate.transpose(0, 2, 1), exp_up.transpose(0, 2, 1), exp_down,
    )


def solution(mesh):
    return jax.shard_map(
        body,
        mesh=mesh,
        in_specs=(
            P("ctx", "exp"),
            P("ctx", "exp"),
            P("ctx", "exp"),
            P("ctx", None),
            P("ctx"),
            P("ctx", None),
            P("ctx", None),
            P("exp", None),
            P(),
            P("exp", "ctx"),
            P("exp", "ctx"),
            P("exp", "ctx"),
            P(("ctx", "exp"), None, None),
            P(("ctx", "exp"), None, None),
            P(("ctx", "exp"), None, None),
        ),
        out_specs=P(("ctx", "exp"), None),
        check_vma=False,
    )
```

```python
import math

import jax
import jax.numpy as jnp
from jax import lax
from jax.experimental import pallas as pl
from jax.experimental.pallas import tpu as pltpu
from jax.sharding import PartitionSpec as P

MESH = pl.DeviceIdType.MESH
HEAD_DIM = 128
NEGATIVE = -1e30
EPSILON = 1e-05
WIDTH = 4096
CHUNK = 1024
CHUNKS = WIDTH // CHUNK
SCALE = WIDTH
WIDE = WIDTH + 128
HALF = CHUNK // 2
PACKED = WIDTH // 2
BF16 = jnp.bfloat16
F32 = jnp.float32


class Place:
    def __init__(self):
        c, e = lax.axis_index("ctx"), lax.axis_index("exp")
        self.e = e
        self.zl, self.x, self.y = lax.div(c, 16), lax.rem(lax.div(c, 4), 4), lax.rem(c, 4)
        self.zh, self.k = lax.div(e, 2), lax.rem(e, 2)
        self.z = self.zh * 2 + self.zl

    def dev(self, dx=0, dy=0, dzl=0, dzh=0, dk=0):
        x, y = lax.rem(self.x + dx + 4, 4), lax.rem(self.y + dy + 4, 4)
        zl, zh, k = lax.rem(self.zl + dzl, 2), lax.rem(self.zh + dzh + 4, 4), lax.rem(self.k + dk, 2)
        return (zl * 16 + x * 4 + y, zh * 2 + k)

    def column(self, dz, core):
        z = lax.rem(self.z + dz + 8, 8)
        return (lax.rem(z, 2) * 16 + self.x * 4 + self.y, lax.div(z, 2) * 2 + core)

    def plane(self, t, back=False):
        dx, dy = lax.div(t, 4), lax.rem(t, 4)
        return self.dev(dx=4 - dx, dy=4 - dy) if back else self.dev(dx=dx, dy=dy)


def remote(src, dst, send, recv, device):
    return pltpu.make_async_remote_copy(
        src_ref=src, dst_ref=dst, send_sem=send, recv_sem=recv, device_id=device, device_id_type=MESH
    )


def nt_dot(a, b):
    return lax.dot_general(a, b, (((1,), (1,)), ((), ())), preferred_element_type=F32)


def tn_dot(a, b):
    return lax.dot_general(a, b, (((0,), (0,)), ((), ())), preferred_element_type=F32)


def pieces(value):
    first = value.astype(BF16).astype(F32)
    second = (value - first).astype(BF16).astype(F32)
    return [first, second, value - first - second]


def active(gate, up):
    return (gate / (1.0 + jnp.exp(-gate)) * up).astype(BF16)


def each(low, high, step):
    def go(t, carried):
        step(t)
        return carried

    lax.fori_loop(low, high, go, 0)


def selection(at, meta, text_map, back_map, image_map):
    lane = lax.broadcasted_iota(jnp.int32, (16, 128), 1)
    spot = lax.broadcasted_iota(jnp.int32, (16, 128), 0)
    to_x = lax.rem(at.x + lax.div(spot, 4), 4)
    to_y = lax.rem(at.y + lax.rem(spot, 4), 4)
    expert = (2 * (at.zl * 16 + to_x * 4 + to_y) + lax.div(at.zh, 2)).astype(F32)
    chosen = jnp.zeros((16, 128), F32)
    gate = jnp.zeros((16, 128), F32)
    for j in range(6):
        hit = jnp.where(meta[j:j + 1, :] == expert, 1.0, 0.0)
        chosen += hit
        gate += hit * meta[6 + j:7 + j, :]
    image = jnp.broadcast_to(meta[12:13, :], (16, 128))
    chosen = jnp.where(image == 0.0, chosen, 0.0)
    gate = jnp.where(image == 0.0, gate, 0.0)
    row = lax.broadcasted_iota(jnp.int32, (128, 128), 0)
    col = lax.broadcasted_iota(jnp.int32, (128, 128), 1)
    earlier = jnp.where((lax.div(row, 16) == lax.div(col, 16)) & (row < col), 1.0, 0.0).astype(BF16)
    rank = jnp.dot(jnp.concatenate([chosen, image], axis=0).astype(BF16), earlier, preferred_element_type=F32)
    sub = lax.div(lane, 16)
    text_slot = jnp.where(chosen > 0.0, (2 * sub).astype(F32) + rank[0:16], -1.0)
    mine = (image > 0.0) & (sub == at.z)
    slot = spot.astype(F32)
    for half in range(2):
        image_slot = jnp.where(mine, rank[16:32] + 8.0 * half, -1.0)
        image_map[half] = jnp.where(image_slot == slot, 1.0, 0.0).astype(BF16)
    for t in range(16):
        match = text_slot[t:t + 1, :] == slot
        text_map[16 * t:16 * t + 16, :] = jnp.where(match, 1.0, 0.0).astype(BF16)
        back_map[16 * t:16 * t + 16, :] = jnp.where(match, gate[t:t + 1, :], 0.0).astype(BF16)


def layer_kernel(
    q_ref, k_ref, v_ref, resid_ref, flags_ref, routes_ref, gates_ref, ow_ref, gain_ref,
    ig_ref, iu_ref, id_ref, eg_ref, eu_ref, ed_ref,
    out_ref,
    kbuf, vbuf, qbuf, obuf, rbuf, ow, res, att, pbuf, sbuf, tbuf, zbuf, state, normed,
    wg, wu, wd, wi, meta, other, text_map, back_map, image_map, rows, tsend, xt, xi, acc,
    ysend, ys, isend, ir1, is2, ir2, zsend, zrecv, zown, spots, spot_recv,
    kv_send, kv_recv, q_send, q_recv, o_send, o_recv, c_send, c_recv, z_send, z_recv, local_sem,
    w_send, w_recv, m_send, m_recv, p_send, p_recv, g_send, g_recv, d_send, d_recv, x1_send, x1_recv, x2_send, x2_recv,
    i_send, i_recv, f_send, f_recv, t_send, t_recv, y1_send, y1_recv, y2_send, y2_recv, e_send, e_recv, s_send, s_recv,
):
    at = Place()
    z, k, zh, zl = at.z, at.k, at.zh, at.zl
    p = lax.rem(zl + k, 2)
    even, odd = p == 0, p == 1
    side_step = 1 - 2 * k
    chunk = [pl.ds(n * CHUNK, CHUNK) for n in range(CHUNKS)]
    size = [CHUNK] * (CHUNKS - 1) + [CHUNK + WIDE - WIDTH]
    wide = [pl.ds(n * CHUNK, size[n]) for n in range(CHUNKS)]
    half = [pl.ds(n * HALF, HALF) for n in range(CHUNKS)]
    packed = [pl.ds(n * HALF, size[n] - HALF) for n in range(CHUNKS)]
    heads = [pl.ds(h * HEAD_DIM, HEAD_DIM) for h in range(2)]

    def load(i, src, dst):
        copy = pltpu.make_async_copy(src, dst, local_sem.at[i])
        copy.start()
        return copy

    own_kv = []
    for h in range(2):
        own_kv.append([
            load(3 * h, q_ref.at[:, heads[h]], qbuf.at[h, 0]),
            load(3 * h + 1, k_ref.at[:, heads[h]], kbuf.at[h, 0]),
            load(3 * h + 2, v_ref.at[:, heads[h]], vbuf.at[h, 0]),
        ])
    own_rows = pl.ds(pl.multiple_of(at.e * 16, 16), 16)
    load_r = load(6, resid_ref.at[own_rows], res)
    load_w = load(7, ow_ref, ow)
    barrier = pltpu.get_barrier_semaphore()
    partners = [at.plane(t) for t in range(1, 16)]
    partners += [at.column(dz, lax.rem(k + dk, 2)) for dz in range(8) for dk in range(2) if (dz, dk) != (0, 0)]
    partners += [at.dev(dzl=1, dy=d) for d in (1, 2, 3)]
    for device in partners:
        pl.semaphore_signal(barrier, inc=1, device_id=device, device_id_type=MESH)
    meta[0:6, :] = routes_ref[...].astype(F32)
    meta[6:12, :] = gates_ref[...].astype(F32)
    meta[12:16, :] = jnp.broadcast_to(flags_ref[...].astype(F32), (4, 128))
    pad = jnp.zeros((4, 512), BF16)
    for i, ref in enumerate((ig_ref, iu_ref, id_ref)):
        wi[zl, at.e, i] = jnp.concatenate([ref[...], pad], axis=0)
    pl.semaphore_wait(barrier, len(partners))

    def q_copy(h, j):
        dy, dzl = lax.rem(j, 4), lax.div(j, 4)
        return remote(q_ref.at[:, heads[h]], qbuf.at[h, j], q_send.at[h, j], q_recv.at[h, j], at.dev(dzl=dzl, dy=dy))

    kv = []
    for h in range(2):
        each(1, 8, lambda j: q_copy(h, j).start())
        kv.append([])
        for d in (1, 3, 2):
            for i, (ref, buf) in enumerate(((k_ref, kbuf), (v_ref, vbuf))):
                copy = remote(ref.at[:, heads[h]], buf.at[h, d], kv_send.at[i, h, d], kv_recv.at[i, h, d], at.dev(dx=d))
                copy.start()
                kv[h].append(copy)
    meta_copy = remote(meta, other, m_send, m_recv, at.dev(dzl=1))
    meta_copy.start()
    weights, swap = [], []
    for i, (src, dst) in enumerate(((eg_ref, wg), (eu_ref, wu), (ed_ref, wd))):
        weights.append(load(8 + i, src.at[0], dst.at[0:352]))
        copy = remote(src.at[0], dst.at[352:704], w_send.at[i], w_recv.at[i], at.dev(dk=1))
        copy.start()
        swap.append(copy)

    def image_slot(dz, core):
        place = lax.rem(z + dz + 8, 8)
        return wi.at[lax.rem(place, 2), lax.div(place, 2) * 2 + core]

    def image_ring(side, i, distance):
        part = image_slot(distance if side else -distance, k)
        if i == 3:
            part = part.at[:, :, 256:512] if side else part.at[:, :, 0:256]
        return remote(part, part, i_send.at[side, i], i_recv.at[side, i], at.column(-1 if side else 1, k))

    def image_pass(dz):
        part = image_slot(dz, k)
        return remote(part, part, f_send.at[dz + 3], f_recv.at[dz + 3], at.dev(dk=1))

    def image_passed(dz):
        part = image_slot(dz, 1 - k)
        return remote(part, part, f_send.at[dz + 3], f_recv.at[dz + 3], at.dev(dk=1))

    def image_step(i):
        for side in range(2):
            image_ring(side, i - 1, i).wait_recv()
            image_ring(side, i, i).start()
            image_pass(i if side else -i).start()

    for side in range(2):
        image_ring(side, 0, 0).start()
    image_pass(0).start()
    key_row = lax.broadcasted_iota(jnp.int32, (512, 128), 0)
    lanes = lax.broadcasted_iota(jnp.int32, (512, 128), 1)
    from_x = lax.rem(at.x - lax.div(key_row, 128) + 4, 4)
    key_spot = (zl * 16 + from_x * 4 + at.y) * 128 + lax.rem(key_row, 128) - lanes

    def back(h, j):
        device = at.dev(dzl=lax.div(j, 4), dy=4 - lax.rem(j, 4))
        return remote(obuf.at[h, j], rbuf.at[h, j], o_send.at[h, j], o_recv.at[h, j], device)

    for h in range(2):
        for copy in own_kv[h]:
            copy.wait()
        for copy in kv[h]:
            copy.wait_recv()

        def one_block(j):
            @pl.when(j > 0)
            def _():
                q_copy(h, j).wait_recv()

            q_zl = lax.rem(zl + lax.div(j, 4), 2)
            q_y = lax.rem(at.y + 4 - lax.rem(j, 4), 4)
            allowed = key_spot <= (q_zl * 16 + at.x * 4 + q_y) * 128
            s = nt_dot(kbuf[h].reshape(512, HEAD_DIM), qbuf[h, j])
            s = jnp.where(allowed, s * (math.log2(math.e) / math.sqrt(HEAD_DIM)), NEGATIVE)
            m = jnp.max(s, axis=0, keepdims=True)
            w = jnp.exp2(s - m)
            l = jnp.sum(w, axis=0, keepdims=True)
            o = tn_dot(vbuf[h].reshape(512, HEAD_DIM), w.astype(BF16))
            obuf[h, j, 0:128, :] = o.astype(BF16)
            stats = pieces(m) + pieces(l) + [m, l]
            obuf[h, j, 128:144, :] = jnp.concatenate(stats + stats, axis=0).astype(BF16)

            @pl.when(j > 0)
            def _():
                back(h, j).start()

        each(0, 8, one_block)


    for h in range(2):
        rbuf[h, 0] = obuf[h, 0]
        for j in range(1, 8):
            back(h, j).wait_recv()
        stats = [rbuf[h, j, 128:144, :].astype(F32) for j in range(8)]
        tops = [st[0:1] + st[1:2] + st[2:3] for st in stats]
        top = tops[0]
        for j in range(1, 8):
            top = jnp.maximum(top, tops[j])
        total = jnp.zeros((HEAD_DIM, 128), F32)
        denom = jnp.zeros((1, 128), F32)
        for j in range(8):
            w = jnp.exp2(tops[j] - top)
            denom += w * (stats[j][3:4] + stats[j][4:5] + stats[j][5:6])
            total += w * rbuf[h, j, 0:128, :].astype(F32)
        att[h * HEAD_DIM:(h + 1) * HEAD_DIM, :] = (total / denom).astype(BF16)

    load_w.wait()
    load_r.wait()
    swaps, sums = [], []
    for n in range(CHUNKS):
        part = tn_dot(att[...], ow[:, chunk[n]]).astype(BF16)
        for b in range(8):
            pbuf[b % 2, b // 2, :, chunk[n]] = part[16 * b:16 * b + 16]
        copy = remote(pbuf.at[1 - k, :, :, chunk[n]], sbuf.at[:, :, chunk[n]], c_send.at[n], c_recv.at[n], at.dev(dk=1))
        copy.start()
        swaps.append(copy)
    for n in range(CHUNKS):
        swaps[n].wait_recv()
        tbuf[:, :, chunk[n]] = (
            pbuf[k, :, :, chunk[n]].astype(F32) + sbuf[:, :, chunk[n]].astype(F32)
        ).astype(BF16)
        for d in (2, 1, 3):
            copy = remote(
                tbuf.at[lax.rem(zh + d, 4), :, chunk[n]], zbuf.at[d - 1, :, chunk[n]],
                z_send.at[n, d], z_recv.at[n, d], at.dev(dzh=d),
            )
            copy.start()
            sums.append(copy)
    meta_copy.wait_recv()
    selection(at, jnp.where(even, meta[...], other[...]), text_map, back_map, image_map)
    powers = []

    def norm_step(n):
        for copy in sums[3 * n:3 * n + 3]:
            copy.wait_recv()
        total = pbuf[k, zh, :, chunk[n]].astype(F32) + sbuf[zh, :, chunk[n]].astype(F32)
        for d in range(3):
            total += zbuf[d, :, chunk[n]].astype(F32)
        total += res[:, chunk[n]].astype(F32)
        state[:, chunk[n]] = total
        powers.append(jnp.sum(total * total, axis=-1, keepdims=True))
        normed[:, chunk[n]] = (total * gain_ref[:, chunk[n]]).astype(BF16)
        if n == CHUNKS - 1:
            scale = jnp.broadcast_to(lax.rsqrt(sum(powers) / WIDTH + EPSILON), (16, 64))
            high = scale.astype(BF16)
            low = (scale - high.astype(F32)).astype(BF16)
            normed[:, SCALE:WIDE] = jnp.concatenate([high, low], axis=1)

        @pl.when(odd)
        def _():
            pair_copy(n).start()

        @pl.when(even)
        def _():
            rows[zh, k, :, wide[n]] = normed[:, wide[n]]
            pair_arrival(n).wait_recv()
            ring_copy(0, 0, n).start()
            ring_copy(1, 0, n).start()

    def pair_copy(n):
        return remote(
            normed.at[:, wide[n]], rows.at[zh, k, :, wide[n]], p_send.at[n], p_recv.at[n], at.dev(dk=1)
        )

    def pair_arrival(n):
        part = rows.at[zh, 1 - k, :, wide[n]]
        return remote(part, part, p_send.at[n], p_recv.at[n], at.dev(dk=1))

    def ring_part(side, steps, n):
        step = steps * side_step
        origin = lax.rem(z - step + 16, 8) if side == 0 else lax.rem(z + step + 16, 8)
        return rows.at[lax.div(origin, 2), :, :, wide[n]]

    def ring_remote(side, i, n, part):
        device = at.column(side_step if side == 0 else -side_step, k)
        return remote(part, part, g_send.at[side, i, n], g_recv.at[side, i, n], device)

    def ring_copy(side, i, n):
        return ring_remote(side, i, n, ring_part(side, 2 * i + p, n))

    def ring_arrival(side, i, n):
        return ring_remote(side, i, n, ring_part(side, 2 * i + 2 - p, n))

    def ring_one(n):
        for side in range(2):
            ring_arrival(side, 0, n).wait_recv()

            @pl.when(even)
            def _():
                ring_copy(side, 1, n).start()

            @pl.when(odd)
            def _():
                ring_copy(side, 0, n).start()

    def ring_two(n):
        ring_arrival(0, 1, n).wait_recv()

        @pl.when(odd)
        def _():
            ring_copy(0, 1, n).start()
            ring_arrival(1, 1, n).wait_recv()

    def text_copy(t, n):
        return remote(tsend.at[t, :, wide[n]], xt.at[t, :, wide[n]], d_send.at[t, n], d_recv.at[t, n], at.plane(t))

    def first_hop(d, n):
        src = xi.at[0, 0, :, packed[n]]
        if n % 2 == 0:
            return remote(src, xi.at[0, d, :, packed[n]], x1_send.at[d, n], x1_recv.at[d, n], at.dev(dx=d))
        return remote(src, xi.at[d, 0, :, packed[n]], x1_send.at[d, n], x1_recv.at[d, n], at.dev(dy=d))

    def second_hop(d, n):
        if n % 2 == 0:
            src, dst, device = xi.at[0, :, :, packed[n]], xi.at[d, :, :, packed[n]], at.dev(dy=d)
        else:
            src, dst, device = xi.at[:, 0, :, packed[n]], xi.at[:, d, :, packed[n]], at.dev(dx=d)
        return remote(src, dst, x2_send.at[d, n], x2_recv.at[d, n], device)

    def dispatch(n):
        part = rows[:, :, :, wide[n]].reshape(128, size[n])
        image = jnp.dot(image_map[0], part[:, 0:HALF], preferred_element_type=F32)
        image += jnp.dot(image_map[1], part[:, HALF:CHUNK], preferred_element_type=F32)
        if size[n] > CHUNK:
            factor = jnp.dot(image_map[0], part[:, CHUNK:], preferred_element_type=F32)
            image = jnp.concatenate([image, factor], axis=1)
        xi[0, 0, :, packed[n]] = image.astype(BF16)
        for d in (1, 3, 2):
            first_hop(d, n).start()
        picked = jnp.dot(text_map[...], part, preferred_element_type=F32).astype(BF16).reshape(16, 16, size[n])
        tsend[:, :, wide[n]] = picked
        xt[0, :, wide[n]] = picked[0]
        each(1, 16, lambda t: text_copy(t, n).start())

    def forward(n):
        for d in (1, 3, 2):
            first_hop(d, n).wait_recv()
        for d in (1, 3, 2):
            second_hop(d, n).start()

    for step in range(CHUNKS + 3):
        if step < CHUNKS:
            norm_step(step)
        if 0 <= step - 1 < CHUNKS:
            ring_one(step - 1)
        if 0 <= step - 2 < CHUNKS:
            ring_two(step - 2)
            if step - 2 == CHUNKS - 1:
                image_step(1)
            dispatch(step - 2)
        if 0 <= step - 3 < CHUNKS:
            forward(step - 3)

    for copy in weights[:2]:
        copy.wait()
    for copy in swap[:2]:
        copy.wait_recv()
    for n in range(CHUNKS):
        each(1, 16, lambda t: text_copy(t, n).wait_recv())
        part = xt[:, :, chunk[n]].reshape(256, CHUNK)
        for i, w in enumerate((wg, wu)):
            term = nt_dot(part, w[:, chunk[n]])
            if n == 0:
                acc[i] = term
            else:
                acc[i] += term
        if n == 1:
            image_step(2)
    text_scale = xt[:, :, SCALE:WIDE].reshape(256, 128).astype(F32)
    text_scale = text_scale[:, 0:1] + text_scale[:, 64:65]
    text_act = active(acc[0] * text_scale, acc[1] * text_scale)
    weights[2].wait()
    swap[2].wait_recv()

    def text_back(t, n):
        return remote(
            ysend.at[t, :, chunk[n]], ys.at[t, :, chunk[n]], t_send.at[t, n], t_recv.at[t, n], at.plane(t, True)
        )

    def text_down(n):
        result = jnp.dot(text_act, wd[:, chunk[n]], preferred_element_type=F32).astype(BF16).reshape(16, 16, CHUNK)
        ysend[:, :, chunk[n]] = result
        ys[0, :, chunk[n]] = result[0]
        each(1, 16, lambda t: text_back(t, n).start())

    image_act = []

    def image_ready():
        for side in range(2):
            image_ring(side, 3, 4).wait_recv()
        image_pass(4).start()
        for dz in (0, -1, 1, -2, 2, -3, 3, 4):
            image_passed(dz).wait_recv()
        lows = [jnp.zeros((256, 352), F32)] * 2
        highs = [jnp.zeros((256, 352), F32)] * 2
        for n in range(CHUNKS):
            for d in (1, 3, 2):
                second_hop(d, n).wait_recv()
            part = xi[:, :, :, half[n]].reshape(256, HALF)
            for b in range(2):
                lows[b] += nt_dot(part, wi[b, 2 * n, 0:2].reshape(352, 512))
                highs[b] += nt_dot(part, wi[b, 2 * n + 1, 0:2].reshape(352, 512))
        image_scale = xi[:, :, :, PACKED:PACKED + 128].reshape(16, 16, 128)[:, 0:8].astype(F32).reshape(128, 128)
        image_scale = image_scale[:, 0:1] + image_scale[:, 64:65]
        for b in range(2):
            gate_up = lows[b].reshape(16, 16, 352)[:, 0:8] + highs[b].reshape(16, 16, 352)[:, 8:16]
            gate_up = gate_up.reshape(128, 352) * image_scale
            image_act.append(active(gate_up[:, 0:176], gate_up[:, 176:352]))

    def sum_one(d, n):
        if n % 2 == 0:
            src, device = isend.at[d, :, :, half[n]], at.dev(dy=4 - d)
        else:
            src, device = isend.at[:, d, :, half[n]], at.dev(dx=4 - d)
        return remote(src, ir1.at[d - 1, :, :, half[n]], y1_send.at[d, n], y1_recv.at[d, n], device)

    def sum_two(d, n):
        device = at.dev(dx=4 - d) if n % 2 == 0 else at.dev(dy=4 - d)
        return remote(is2.at[d, :, half[n]], ir2.at[d - 1, :, half[n]], y2_send.at[d, n], y2_recv.at[d, n], device)

    def image_down(n):
        parts = []
        for e in (2 * n, 2 * n + 1):
            result = sum(jnp.dot(image_act[b], wi[b, e, 2], preferred_element_type=F32) for b in range(2))
            parts.append(result.reshape(16, 8, HALF))
        isend[:, :, :, half[n]] = jnp.concatenate(parts, axis=1).astype(BF16).reshape(4, 4, 16, HALF)
        for d in (1, 3, 2):
            sum_one(d, n).start()

    def image_turn(n):
        total = (isend[0, :, :, half[n]] if n % 2 == 0 else isend[:, 0, :, half[n]]).astype(F32)
        for d in (1, 3, 2):
            sum_one(d, n).wait_recv()
            total += ir1[d - 1, :, :, half[n]].astype(F32)
        is2[:, :, half[n]] = total.astype(BF16)
        for d in (1, 3, 2):
            sum_two(d, n).start()

    def to_owner(i, core, n):
        dz = p + 2 * i
        target = lax.div(lax.rem(z + dz, 8), 2) * 2 + core
        return remote(
            zsend.at[target, :, chunk[n]], zrecv.at[dz, :, chunk[n]],
            e_send.at[i, core, n], e_recv.at[dz, n], at.column(dz, core),
        )

    def from_column(dz, n):
        part = zrecv.at[dz, :, chunk[n]]
        return remote(part, part, e_send.at[0, 0, n], e_recv.at[dz, n], at.column(dz, k))

    def combine(n):
        each(1, 16, lambda t: text_back(t, n).wait_recv())
        total = tn_dot(back_map[...], ys[:, :, chunk[n]].reshape(256, CHUNK))
        total = total.reshape(8, 16, CHUNK)
        zsend[:, :, chunk[n]] = total.astype(BF16)
        for i in (2, 1, 3):
            for core in range(2):
                to_owner(i, core, n).start()

        @pl.when(odd)
        def _():
            for core in range(2):
                to_owner(0, core, n).start()

        @pl.when(even)
        def _():
            to_owner(0, 1 - k, n).start()
            zown[:, chunk[n]] = zsend[at.e, :, chunk[n]].astype(F32)

        @pl.when(odd)
        def _():
            zown[:, chunk[n]] = jnp.zeros((16, CHUNK), F32)

    def finish(n):
        total = state[:, chunk[n]] + zown[:, chunk[n]]
        for dz in range(1, 8):
            from_column(dz, n).wait_recv()
            total += zrecv[dz, :, chunk[n]].astype(F32)
        state[:, chunk[n]] = total

        @pl.when(odd)
        def _():
            from_column(0, n).wait_recv()
            state[:, chunk[n]] = total + zrecv[0, :, chunk[n]].astype(F32)

    def spot_swap(n):
        return remote(
            spots.at[z, :, chunk[n]], spot_recv.at[:, chunk[n]], s_send.at[n], s_recv.at[n], at.dev(dzl=1, dk=1)
        )

    def image_out(n):
        image_total = is2[0, :, half[n]].astype(F32)
        for d in (1, 3, 2):
            sum_two(d, n).wait_recv()
            image_total += ir2[d - 1, :, half[n]].astype(F32)
        image_total = image_total.astype(BF16)
        spread = jnp.concatenate([tn_dot(image_map[b], image_total) for b in range(2)], axis=1)
        spots[:, :, chunk[n]] = spread.astype(BF16).reshape(8, 16, CHUNK)

        @pl.when(odd)
        def _():
            spot_swap(n).start()

    def image_end(n):
        @pl.when(even)
        def _():
            out_ref[:, chunk[n]] = (state[:, chunk[n]] + spots[z, :, chunk[n]].astype(F32)).astype(BF16)

        @pl.when(odd)
        def _():
            spot_swap(n).wait_recv()
            out_ref[:, chunk[n]] = (state[:, chunk[n]] + spot_recv[:, chunk[n]].astype(F32)).astype(BF16)

    text_down(0)
    text_down(1)
    text_down(2)
    text_down(3)
    image_step(3)
    combine(0)
    combine(1)
    image_ready()
    image_down(0)
    image_down(1)
    image_down(2)
    image_down(3)
    combine(2)
    finish(0)
    image_turn(0)
    image_turn(1)
    combine(3)
    finish(1)
    image_turn(2)
    image_turn(3)
    image_out(0)
    finish(2)
    image_out(1)
    image_end(0)
    image_out(2)
    image_end(1)
    image_out(3)
    image_end(2)
    finish(3)
    image_end(3)

    meta_copy.wait_send()
    for copy in kv[0] + kv[1] + swap + swaps + sums:
        copy.wait_send()
    for h in range(2):
        def sent_a(j):
            q_copy(h, j).wait_send()
            back(h, j).wait_send()

        each(1, 8, sent_a)
    for dz in range(-3, 5):
        image_pass(dz).wait_send()
    for i in range(4):
        for side in range(2):
            image_ring(side, i, i).wait_send()
    for n in range(CHUNKS):
        def sent_b(t):
            text_copy(t, n).wait_send()
            text_back(t, n).wait_send()

        each(1, 16, sent_b)
        for d in (1, 2, 3):
            first_hop(d, n).wait_send()
            second_hop(d, n).wait_send()
            sum_one(d, n).wait_send()
            sum_two(d, n).wait_send()
            for core in range(2):
                to_owner(d, core, n).wait_send()

        for side, i in ((0, 0), (1, 0), (0, 1)):
            ring_copy(side, i, n).wait_send()

        @pl.when(odd)
        def _():
            pair_copy(n).wait_send()
            spot_swap(n).wait_send()
            for core in range(2):
                to_owner(0, core, n).wait_send()

        @pl.when(even)
        def _():
            ring_copy(1, 1, n).wait_send()
            to_owner(0, 1 - k, n).wait_send()


def body(
    query, keys, values, resid, flags, routes, gates, out_weight, norm_gain,
    img_gate, img_up, img_down, exp_gate, exp_up, exp_down,
):
    vmem, hbm = pl.BlockSpec(memory_space=pltpu.VMEM), pl.BlockSpec(memory_space=pl.ANY)
    dma = pltpu.SemaphoreType.DMA

    def buf(*shape, dtype=BF16):
        return pltpu.VMEM(shape, dtype)

    def pair(*shape):
        return [dma(shape), dma(shape)]

    return pl.pallas_call(
        layer_kernel,
        name="layer",
        out_shape=jax.ShapeDtypeStruct((16, WIDTH), BF16),
        in_specs=[hbm] * 4 + [vmem] * 3 + [hbm, vmem] + [vmem] * 3 + [hbm] * 3,
        out_specs=vmem,
        scratch_shapes=[
            buf(2, 4, 128, 128), buf(2, 4, 128, 128), buf(2, 8, 128, 128), buf(2, 8, 144, 128), buf(2, 8, 144, 128),
            buf(256, WIDTH), buf(16, WIDTH), buf(256, 128),
            buf(2, 4, 16, WIDTH), buf(4, 16, WIDTH), buf(4, 16, WIDTH), buf(3, 16, WIDTH),
            buf(16, WIDTH, dtype=F32), buf(16, WIDE),
            buf(704, WIDTH), buf(704, WIDTH), buf(704, WIDTH), buf(2, 8, 3, 176, 512),
            buf(16, 128, dtype=F32), buf(16, 128, dtype=F32), buf(256, 128), buf(256, 128), buf(2, 16, 128),
            buf(4, 2, 16, WIDE), buf(16, 16, WIDE), buf(16, 16, WIDE), buf(4, 4, 16, PACKED + 128),
            buf(2, 256, 704, dtype=F32),
            buf(16, 16, WIDTH), buf(16, 16, WIDTH), buf(4, 4, 16, PACKED), buf(3, 4, 16, PACKED),
            buf(4, 16, PACKED), buf(3, 16, PACKED), buf(8, 16, WIDTH), buf(8, 16, WIDTH), buf(16, WIDTH, dtype=F32), buf(8, 16, WIDTH), buf(16, WIDTH),
            *pair(2, 2, 4), *pair(2, 8), *pair(2, 8), *pair(CHUNKS), *pair(CHUNKS, 4), dma((11,)),
            *pair(3), dma, dma, *pair(CHUNKS), *pair(2, 2, CHUNKS), *pair(16, CHUNKS),
            *pair(4, CHUNKS), *pair(4, CHUNKS), *pair(2, 4), *pair(8), *pair(16, CHUNKS),
            *pair(4, CHUNKS), *pair(4, CHUNKS), dma((4, 2, CHUNKS)), dma((8, CHUNKS)), *pair(CHUNKS),
        ],
        compiler_params=pltpu.CompilerParams(
            collective_id=1, has_side_effects=True, vmem_limit_bytes=60 << 20
        ),
    )(
        query, keys, values, resid, flags.reshape(1, -1), routes.T, gates.T, out_weight, norm_gain.reshape(1, WIDTH),
        img_gate.T, img_up.T, img_down.T,
        exp_gate.transpose(0, 2, 1), exp_up.transpose(0, 2, 1), exp_down,
    )


def solution(mesh):
    return jax.shard_map(
        body,
        mesh=mesh,
        in_specs=(
            P("ctx", "exp"),
            P("ctx", "exp"),
            P("ctx", "exp"),
            P("ctx", None),
            P("ctx"),
            P("ctx", None),
            P("ctx", None),
            P("exp", None),
            P(),
            P("exp", "ctx"),
            P("exp", "ctx"),
            P("exp", "ctx"),
            P(("ctx", "exp"), None, None),
            P(("ctx", "exp"), None, None),
            P(("ctx", "exp"), None, None),
        ),
        out_specs=P(("ctx", "exp"), None),
        check_vma=False,
    )
```

```python
import math

import jax
import jax.numpy as jnp
from jax import lax
from jax.experimental import pallas as pl
from jax.experimental.pallas import tpu as pltpu
from jax.sharding import PartitionSpec as P

MESH = pl.DeviceIdType.MESH
HEAD_DIM = 128
NEGATIVE = -1e30
EPSILON = 1e-05
WIDTH = 4096
CHUNK = 1024
CHUNKS = WIDTH // CHUNK
SCALE = WIDTH
WIDE = WIDTH + 128
HALF = CHUNK // 2
PACKED = WIDTH // 2
BF16 = jnp.bfloat16
F32 = jnp.float32


class Place:
    def __init__(self):
        c, e = lax.axis_index("ctx"), lax.axis_index("exp")
        self.e = e
        self.zl, self.x, self.y = lax.div(c, 16), lax.rem(lax.div(c, 4), 4), lax.rem(c, 4)
        self.zh, self.k = lax.div(e, 2), lax.rem(e, 2)
        self.z = self.zh * 2 + self.zl

    def dev(self, dx=0, dy=0, dzl=0, dzh=0, dk=0):
        x, y = lax.rem(self.x + dx + 4, 4), lax.rem(self.y + dy + 4, 4)
        zl, zh, k = lax.rem(self.zl + dzl, 2), lax.rem(self.zh + dzh + 4, 4), lax.rem(self.k + dk, 2)
        return (zl * 16 + x * 4 + y, zh * 2 + k)

    def column(self, dz, core):
        z = lax.rem(self.z + dz + 8, 8)
        return (lax.rem(z, 2) * 16 + self.x * 4 + self.y, lax.div(z, 2) * 2 + core)

    def plane(self, t, back=False):
        dx, dy = lax.div(t, 4), lax.rem(t, 4)
        return self.dev(dx=4 - dx, dy=4 - dy) if back else self.dev(dx=dx, dy=dy)


def remote(src, dst, send, recv, device):
    return pltpu.make_async_remote_copy(
        src_ref=src, dst_ref=dst, send_sem=send, recv_sem=recv, device_id=device, device_id_type=MESH
    )


def nt_dot(a, b):
    return lax.dot_general(a, b, (((1,), (1,)), ((), ())), preferred_element_type=F32)


def tn_dot(a, b):
    return lax.dot_general(a, b, (((0,), (0,)), ((), ())), preferred_element_type=F32)


def pieces(value):
    first = value.astype(BF16).astype(F32)
    second = (value - first).astype(BF16).astype(F32)
    return [first, second, value - first - second]


def active(gate, up):
    return (gate / (1.0 + jnp.exp(-gate)) * up).astype(BF16)


def each(low, high, step):
    def go(t, carried):
        step(t)
        return carried

    lax.fori_loop(low, high, go, 0)


def selection(at, meta, text_map, back_map, image_map):
    lane = lax.broadcasted_iota(jnp.int32, (16, 128), 1)
    spot = lax.broadcasted_iota(jnp.int32, (16, 128), 0)
    to_x = lax.rem(at.x + lax.div(spot, 4), 4)
    to_y = lax.rem(at.y + lax.rem(spot, 4), 4)
    expert = (2 * (at.zl * 16 + to_x * 4 + to_y) + lax.div(at.zh, 2)).astype(F32)
    chosen = jnp.zeros((16, 128), F32)
    gate = jnp.zeros((16, 128), F32)
    for j in range(6):
        hit = jnp.where(meta[j:j + 1, :] == expert, 1.0, 0.0)
        chosen += hit
        gate += hit * meta[6 + j:7 + j, :]
    image = jnp.broadcast_to(meta[12:13, :], (16, 128))
    chosen = jnp.where(image == 0.0, chosen, 0.0)
    gate = jnp.where(image == 0.0, gate, 0.0)
    row = lax.broadcasted_iota(jnp.int32, (128, 128), 0)
    col = lax.broadcasted_iota(jnp.int32, (128, 128), 1)
    earlier = jnp.where((lax.div(row, 16) == lax.div(col, 16)) & (row < col), 1.0, 0.0).astype(BF16)
    rank = jnp.dot(jnp.concatenate([chosen, image], axis=0).astype(BF16), earlier, preferred_element_type=F32)
    sub = lax.div(lane, 16)
    text_slot = jnp.where(chosen > 0.0, (2 * sub).astype(F32) + rank[0:16], -1.0)
    mine = (image > 0.0) & (sub == at.z)
    slot = spot.astype(F32)
    for half in range(2):
        image_slot = jnp.where(mine, rank[16:32] + 8.0 * half, -1.0)
        image_map[half] = jnp.where(image_slot == slot, 1.0, 0.0).astype(BF16)
    for t in range(16):
        match = text_slot[t:t + 1, :] == slot
        text_map[16 * t:16 * t + 16, :] = jnp.where(match, 1.0, 0.0).astype(BF16)
        back_map[16 * t:16 * t + 16, :] = jnp.where(match, gate[t:t + 1, :], 0.0).astype(BF16)


def layer_kernel(
    q_ref, k_ref, v_ref, resid_ref, flags_ref, routes_ref, gates_ref, ow_ref, gain_ref,
    ig_ref, iu_ref, id_ref, eg_ref, eu_ref, ed_ref,
    out_ref,
    kbuf, vbuf, qbuf, obuf, rbuf, ow, res, att, pbuf, sbuf, tbuf, zbuf, state, normed,
    wg, wu, wd, wi, meta, other, text_map, back_map, image_map, rows, tsend, xt, xi, acc,
    ysend, ys, isend, ir1, is2, ir2, zsend, zrecv, zown, spots, spot_recv,
    kv_send, kv_recv, q_send, q_recv, o_send, o_recv, c_send, c_recv, z_send, z_recv, local_sem,
    w_send, w_recv, m_send, m_recv, p_send, p_recv, g_send, g_recv, d_send, d_recv, x1_send, x1_recv, x2_send, x2_recv,
    i_send, i_recv, f_send, f_recv, t_send, t_recv, y1_send, y1_recv, y2_send, y2_recv, e_send, e_recv, s_send, s_recv,
):
    at = Place()
    z, k, zh, zl = at.z, at.k, at.zh, at.zl
    p = lax.rem(zl + k, 2)
    even, odd = p == 0, p == 1
    side_step = 1 - 2 * k
    chunk = [pl.ds(n * CHUNK, CHUNK) for n in range(CHUNKS)]
    size = [CHUNK] * (CHUNKS - 1) + [CHUNK + WIDE - WIDTH]
    wide = [pl.ds(n * CHUNK, size[n]) for n in range(CHUNKS)]
    half = [pl.ds(n * HALF, HALF) for n in range(CHUNKS)]
    packed = [pl.ds(n * HALF, size[n] - HALF) for n in range(CHUNKS)]
    heads = [pl.ds(h * HEAD_DIM, HEAD_DIM) for h in range(2)]

    def load(i, src, dst):
        copy = pltpu.make_async_copy(src, dst, local_sem.at[i])
        copy.start()
        return copy

    own_kv = []
    for h in range(2):
        own_kv.append([
            load(3 * h, q_ref.at[:, heads[h]], qbuf.at[h, 0]),
            load(3 * h + 1, k_ref.at[:, heads[h]], kbuf.at[h, 0]),
            load(3 * h + 2, v_ref.at[:, heads[h]], vbuf.at[h, 0]),
        ])
    own_rows = pl.ds(pl.multiple_of(at.e * 16, 16), 16)
    load_r = load(6, resid_ref.at[own_rows], res)
    load_w = load(7, ow_ref, ow)
    barrier = pltpu.get_barrier_semaphore()
    partners = [at.plane(t) for t in range(1, 16)]
    partners += [at.column(dz, lax.rem(k + dk, 2)) for dz in range(8) for dk in range(2) if (dz, dk) != (0, 0)]
    partners += [at.dev(dzl=1, dy=d) for d in (1, 2, 3)]
    for device in partners:
        pl.semaphore_signal(barrier, inc=1, device_id=device, device_id_type=MESH)
    meta[0:6, :] = routes_ref[...].astype(F32)
    meta[6:12, :] = gates_ref[...].astype(F32)
    meta[12:16, :] = jnp.broadcast_to(flags_ref[...].astype(F32), (4, 128))
    pad = jnp.zeros((4, 512), BF16)
    for i, ref in enumerate((ig_ref, iu_ref, id_ref)):
        wi[zl, at.e, i] = jnp.concatenate([ref[...], pad], axis=0)
    pl.semaphore_wait(barrier, len(partners))

    def q_copy(h, j):
        dy, dzl = lax.rem(j, 4), lax.div(j, 4)
        return remote(q_ref.at[:, heads[h]], qbuf.at[h, j], q_send.at[h, j], q_recv.at[h, j], at.dev(dzl=dzl, dy=dy))

    kv = []
    for h in range(2):
        each(1, 8, lambda j: q_copy(h, j).start())
        kv.append([])
        for d in (1, 3, 2):
            for i, (ref, buf) in enumerate(((k_ref, kbuf), (v_ref, vbuf))):
                copy = remote(ref.at[:, heads[h]], buf.at[h, d], kv_send.at[i, h, d], kv_recv.at[i, h, d], at.dev(dx=d))
                copy.start()
                kv[h].append(copy)
    meta_copy = remote(meta, other, m_send, m_recv, at.dev(dzl=1))
    meta_copy.start()
    weights, swap = [], []
    for i, (src, dst) in enumerate(((eg_ref, wg), (eu_ref, wu), (ed_ref, wd))):
        weights.append(load(8 + i, src.at[0], dst.at[0:352]))
        copy = remote(src.at[0], dst.at[352:704], w_send.at[i], w_recv.at[i], at.dev(dk=1))
        copy.start()
        swap.append(copy)

    def image_slot(dz, core):
        place = lax.rem(z + dz + 8, 8)
        return wi.at[lax.rem(place, 2), lax.div(place, 2) * 2 + core]

    def image_ring(side, i, distance):
        part = image_slot(distance if side else -distance, k)
        if i == 3:
            part = part.at[:, :, 256:512] if side else part.at[:, :, 0:256]
        return remote(part, part, i_send.at[side, i], i_recv.at[side, i], at.column(-1 if side else 1, k))

    def image_pass(dz):
        part = image_slot(dz, k)
        return remote(part, part, f_send.at[dz + 3], f_recv.at[dz + 3], at.dev(dk=1))

    def image_passed(dz):
        part = image_slot(dz, 1 - k)
        return remote(part, part, f_send.at[dz + 3], f_recv.at[dz + 3], at.dev(dk=1))

    def image_step(i):
        for side in range(2):
            image_ring(side, i - 1, i).wait_recv()
            image_ring(side, i, i).start()
            image_pass(i if side else -i).start()

    for side in range(2):
        image_ring(side, 0, 0).start()
    image_pass(0).start()
    key_row = lax.broadcasted_iota(jnp.int32, (512, 128), 0)
    lanes = lax.broadcasted_iota(jnp.int32, (512, 128), 1)
    from_x = lax.rem(at.x - lax.div(key_row, 128) + 4, 4)
    key_spot = (zl * 16 + from_x * 4 + at.y) * 128 + lax.rem(key_row, 128) - lanes

    def back(h, j):
        device = at.dev(dzl=lax.div(j, 4), dy=4 - lax.rem(j, 4))
        return remote(obuf.at[h, j], rbuf.at[h, j], o_send.at[h, j], o_recv.at[h, j], device)

    for h in range(2):
        for copy in own_kv[h]:
            copy.wait()
        for copy in kv[h]:
            copy.wait_recv()

        def one_block(j):
            @pl.when(j > 0)
            def _():
                q_copy(h, j).wait_recv()

            q_zl = lax.rem(zl + lax.div(j, 4), 2)
            q_y = lax.rem(at.y + 4 - lax.rem(j, 4), 4)
            allowed = key_spot <= (q_zl * 16 + at.x * 4 + q_y) * 128
            s = nt_dot(kbuf[h].reshape(512, HEAD_DIM), qbuf[h, j])
            s = jnp.where(allowed, s * (math.log2(math.e) / math.sqrt(HEAD_DIM)), NEGATIVE)
            m = jnp.max(s, axis=0, keepdims=True)
            w = jnp.exp2(s - m)
            l = jnp.sum(w, axis=0, keepdims=True)
            o = tn_dot(vbuf[h].reshape(512, HEAD_DIM), w.astype(BF16))
            obuf[h, j, 0:128, :] = o.astype(BF16)
            stats = pieces(m) + pieces(l) + [m, l]
            obuf[h, j, 128:144, :] = jnp.concatenate(stats + stats, axis=0).astype(BF16)

            @pl.when(j > 0)
            def _():
                back(h, j).start()

        each(0, 8, one_block)


    for h in range(2):
        rbuf[h, 0] = obuf[h, 0]
        for j in range(1, 8):
            back(h, j).wait_recv()
        stats = [rbuf[h, j, 128:144, :].astype(F32) for j in range(8)]
        tops = [st[0:1] + st[1:2] + st[2:3] for st in stats]
        top = tops[0]
        for j in range(1, 8):
            top = jnp.maximum(top, tops[j])
        total = jnp.zeros((HEAD_DIM, 128), F32)
        denom = jnp.zeros((1, 128), F32)
        for j in range(8):
            w = jnp.exp2(tops[j] - top)
            denom += w * (stats[j][3:4] + stats[j][4:5] + stats[j][5:6])
            total += w * rbuf[h, j, 0:128, :].astype(F32)
        att[h * HEAD_DIM:(h + 1) * HEAD_DIM, :] = (total / denom).astype(BF16)

    load_w.wait()
    load_r.wait()
    swaps, sums = [], []
    for n in range(CHUNKS):
        part = tn_dot(att[...], ow[:, chunk[n]]).astype(BF16)
        for b in range(8):
            pbuf[b % 2, b // 2, :, chunk[n]] = part[16 * b:16 * b + 16]
        copy = remote(pbuf.at[1 - k, :, :, chunk[n]], sbuf.at[:, :, chunk[n]], c_send.at[n], c_recv.at[n], at.dev(dk=1))
        copy.start()
        swaps.append(copy)
    for n in range(CHUNKS):
        swaps[n].wait_recv()
        tbuf[:, :, chunk[n]] = (
            pbuf[k, :, :, chunk[n]].astype(F32) + sbuf[:, :, chunk[n]].astype(F32)
        ).astype(BF16)
        for d in (2, 1, 3):
            copy = remote(
                tbuf.at[lax.rem(zh + d, 4), :, chunk[n]], zbuf.at[d - 1, :, chunk[n]],
                z_send.at[n, d], z_recv.at[n, d], at.dev(dzh=d),
            )
            copy.start()
            sums.append(copy)
    meta_copy.wait_recv()
    selection(at, jnp.where(even, meta[...], other[...]), text_map, back_map, image_map)
    powers = []

    def norm_step(n):
        for copy in sums[3 * n:3 * n + 3]:
            copy.wait_recv()
        total = pbuf[k, zh, :, chunk[n]].astype(F32) + sbuf[zh, :, chunk[n]].astype(F32)
        for d in range(3):
            total += zbuf[d, :, chunk[n]].astype(F32)
        total += res[:, chunk[n]].astype(F32)
        state[:, chunk[n]] = total
        powers.append(jnp.sum(total * total, axis=-1, keepdims=True))
        normed[:, chunk[n]] = (total * gain_ref[:, chunk[n]]).astype(BF16)
        if n == CHUNKS - 1:
            scale = jnp.broadcast_to(lax.rsqrt(sum(powers) / WIDTH + EPSILON), (16, 64))
            high = scale.astype(BF16)
            low = (scale - high.astype(F32)).astype(BF16)
            normed[:, SCALE:WIDE] = jnp.concatenate([high, low], axis=1)

        @pl.when(odd)
        def _():
            pair_copy(n).start()

        @pl.when(even)
        def _():
            rows[zh, k, :, wide[n]] = normed[:, wide[n]]
            pair_arrival(n).wait_recv()
            ring_copy(0, 0, n).start()
            ring_copy(1, 0, n).start()

    def pair_copy(n):
        return remote(
            normed.at[:, wide[n]], rows.at[zh, k, :, wide[n]], p_send.at[n], p_recv.at[n], at.dev(dk=1)
        )

    def pair_arrival(n):
        part = rows.at[zh, 1 - k, :, wide[n]]
        return remote(part, part, p_send.at[n], p_recv.at[n], at.dev(dk=1))

    def ring_part(side, steps, n):
        step = steps * side_step
        origin = lax.rem(z - step + 16, 8) if side == 0 else lax.rem(z + step + 16, 8)
        return rows.at[lax.div(origin, 2), :, :, wide[n]]

    def ring_remote(side, i, n, part):
        device = at.column(side_step if side == 0 else -side_step, k)
        return remote(part, part, g_send.at[side, i, n], g_recv.at[side, i, n], device)

    def ring_copy(side, i, n):
        return ring_remote(side, i, n, ring_part(side, 2 * i + p, n))

    def ring_arrival(side, i, n):
        return ring_remote(side, i, n, ring_part(side, 2 * i + 2 - p, n))

    def ring_one(n):
        for side in range(2):
            ring_arrival(side, 0, n).wait_recv()

            @pl.when(even)
            def _():
                ring_copy(side, 1, n).start()

            @pl.when(odd)
            def _():
                ring_copy(side, 0, n).start()

    def ring_two(n):
        ring_arrival(0, 1, n).wait_recv()

        @pl.when(odd)
        def _():
            ring_copy(0, 1, n).start()
            ring_arrival(1, 1, n).wait_recv()

    def text_copy(t, n):
        return remote(tsend.at[t, :, wide[n]], xt.at[t, :, wide[n]], d_send.at[t, n], d_recv.at[t, n], at.plane(t))

    def first_hop(d, n):
        src = xi.at[0, 0, :, packed[n]]
        if n % 2 == 0:
            return remote(src, xi.at[0, d, :, packed[n]], x1_send.at[d, n], x1_recv.at[d, n], at.dev(dx=d))
        return remote(src, xi.at[d, 0, :, packed[n]], x1_send.at[d, n], x1_recv.at[d, n], at.dev(dy=d))

    def second_hop(d, n):
        if n % 2 == 0:
            src, dst, device = xi.at[0, :, :, packed[n]], xi.at[d, :, :, packed[n]], at.dev(dy=d)
        else:
            src, dst, device = xi.at[:, 0, :, packed[n]], xi.at[:, d, :, packed[n]], at.dev(dx=d)
        return remote(src, dst, x2_send.at[d, n], x2_recv.at[d, n], device)

    def dispatch(n):
        part = rows[:, :, :, wide[n]].reshape(128, size[n])
        image = jnp.dot(image_map[0], part[:, 0:HALF], preferred_element_type=F32)
        image += jnp.dot(image_map[1], part[:, HALF:CHUNK], preferred_element_type=F32)
        if size[n] > CHUNK:
            factor = jnp.dot(image_map[0], part[:, CHUNK:], preferred_element_type=F32)
            image = jnp.concatenate([image, factor], axis=1)
        xi[0, 0, :, packed[n]] = image.astype(BF16)
        for d in (1, 3, 2):
            first_hop(d, n).start()
        picked = jnp.dot(text_map[...], part, preferred_element_type=F32).astype(BF16).reshape(16, 16, size[n])
        tsend[:, :, wide[n]] = picked
        xt[0, :, wide[n]] = picked[0]
        each(1, 16, lambda t: text_copy(t, n).start())

    def forward(n):
        for d in (1, 3, 2):
            first_hop(d, n).wait_recv()
        for d in (1, 3, 2):
            second_hop(d, n).start()

    for step in range(CHUNKS + 2):
        if step < CHUNKS:
            norm_step(step)
        if 0 <= step - 1 < CHUNKS:
            ring_one(step - 1)
        if 0 <= step - 2 < CHUNKS:
            ring_two(step - 2)
            if step - 2 == CHUNKS - 1:
                image_step(1)
            dispatch(step - 2)

    for n in range(CHUNKS):
        forward(n)
    for copy in weights[:2]:
        copy.wait()
    for copy in swap[:2]:
        copy.wait_recv()
    for n in range(CHUNKS):
        each(1, 16, lambda t: text_copy(t, n).wait_recv())
        part = xt[:, :, chunk[n]].reshape(256, CHUNK)
        for i, w in enumerate((wg, wu)):
            term = nt_dot(part, w[:, chunk[n]])
            if n == 0:
                acc[i] = term
            else:
                acc[i] += term
        if n == 0:
            image_step(2)
    text_scale = xt[:, :, SCALE:WIDE].reshape(256, 128).astype(F32)
    text_scale = text_scale[:, 0:1] + text_scale[:, 64:65]
    text_act = active(acc[0] * text_scale, acc[1] * text_scale)
    weights[2].wait()
    swap[2].wait_recv()

    def text_back(t, n):
        return remote(
            ysend.at[t, :, chunk[n]], ys.at[t, :, chunk[n]], t_send.at[t, n], t_recv.at[t, n], at.plane(t, True)
        )

    def text_down(n):
        result = jnp.dot(text_act, wd[:, chunk[n]], preferred_element_type=F32).astype(BF16).reshape(16, 16, CHUNK)
        ysend[:, :, chunk[n]] = result
        ys[0, :, chunk[n]] = result[0]
        each(1, 16, lambda t: text_back(t, n).start())

    image_act = []

    def image_ready():
        for side in range(2):
            image_ring(side, 3, 4).wait_recv()
        image_pass(4).start()
        for dz in (0, -1, 1, -2, 2, -3, 3, 4):
            image_passed(dz).wait_recv()
        lows = [jnp.zeros((256, 352), F32)] * 2
        highs = [jnp.zeros((256, 352), F32)] * 2
        for n in range(CHUNKS):
            for d in (1, 3, 2):
                second_hop(d, n).wait_recv()
            part = xi[:, :, :, half[n]].reshape(256, HALF)
            for b in range(2):
                lows[b] += nt_dot(part, wi[b, 2 * n, 0:2].reshape(352, 512))
                highs[b] += nt_dot(part, wi[b, 2 * n + 1, 0:2].reshape(352, 512))
        image_scale = xi[:, :, :, PACKED:PACKED + 128].reshape(16, 16, 128)[:, 0:8].astype(F32).reshape(128, 128)
        image_scale = image_scale[:, 0:1] + image_scale[:, 64:65]
        for b in range(2):
            gate_up = lows[b].reshape(16, 16, 352)[:, 0:8] + highs[b].reshape(16, 16, 352)[:, 8:16]
            gate_up = gate_up.reshape(128, 352) * image_scale
            image_act.append(active(gate_up[:, 0:176], gate_up[:, 176:352]))

    def sum_one(d, n):
        if n % 2 == 0:
            src, device = isend.at[d, :, :, half[n]], at.dev(dy=4 - d)
        else:
            src, device = isend.at[:, d, :, half[n]], at.dev(dx=4 - d)
        return remote(src, ir1.at[d - 1, :, :, half[n]], y1_send.at[d, n], y1_recv.at[d, n], device)

    def sum_two(d, n):
        device = at.dev(dx=4 - d) if n % 2 == 0 else at.dev(dy=4 - d)
        return remote(is2.at[d, :, half[n]], ir2.at[d - 1, :, half[n]], y2_send.at[d, n], y2_recv.at[d, n], device)

    def image_down(n):
        parts = []
        for e in (2 * n, 2 * n + 1):
            result = sum(jnp.dot(image_act[b], wi[b, e, 2], preferred_element_type=F32) for b in range(2))
            parts.append(result.reshape(16, 8, HALF))
        isend[:, :, :, half[n]] = jnp.concatenate(parts, axis=1).astype(BF16).reshape(4, 4, 16, HALF)
        for d in (1, 3, 2):
            sum_one(d, n).start()

    def image_turn(n):
        total = (isend[0, :, :, half[n]] if n % 2 == 0 else isend[:, 0, :, half[n]]).astype(F32)
        for d in (1, 3, 2):
            sum_one(d, n).wait_recv()
            total += ir1[d - 1, :, :, half[n]].astype(F32)
        is2[:, :, half[n]] = total.astype(BF16)
        for d in (1, 3, 2):
            sum_two(d, n).start()

    def to_owner(i, core, n):
        dz = p + 2 * i
        target = lax.div(lax.rem(z + dz, 8), 2) * 2 + core
        return remote(
            zsend.at[target, :, chunk[n]], zrecv.at[dz, :, chunk[n]],
            e_send.at[i, core, n], e_recv.at[dz, n], at.column(dz, core),
        )

    def from_column(dz, n):
        part = zrecv.at[dz, :, chunk[n]]
        return remote(part, part, e_send.at[0, 0, n], e_recv.at[dz, n], at.column(dz, k))

    def combine(n):
        each(1, 16, lambda t: text_back(t, n).wait_recv())
        total = tn_dot(back_map[...], ys[:, :, chunk[n]].reshape(256, CHUNK))
        total = total.reshape(8, 16, CHUNK)
        zsend[:, :, chunk[n]] = total.astype(BF16)
        for i in (2, 1, 3):
            for core in range(2):
                to_owner(i, core, n).start()

        @pl.when(odd)
        def _():
            for core in range(2):
                to_owner(0, core, n).start()

        @pl.when(even)
        def _():
            to_owner(0, 1 - k, n).start()
            zown[:, chunk[n]] = zsend[at.e, :, chunk[n]].astype(F32)

        @pl.when(odd)
        def _():
            zown[:, chunk[n]] = jnp.zeros((16, CHUNK), F32)

    def finish(n):
        total = state[:, chunk[n]] + zown[:, chunk[n]]
        for dz in range(1, 8):
            from_column(dz, n).wait_recv()
            total += zrecv[dz, :, chunk[n]].astype(F32)
        state[:, chunk[n]] = total

        @pl.when(odd)
        def _():
            from_column(0, n).wait_recv()
            state[:, chunk[n]] = total + zrecv[0, :, chunk[n]].astype(F32)

    def spot_swap(n):
        return remote(
            spots.at[z, :, chunk[n]], spot_recv.at[:, chunk[n]], s_send.at[n], s_recv.at[n], at.dev(dzl=1, dk=1)
        )

    def image_out(n):
        image_total = is2[0, :, half[n]].astype(F32)
        for d in (1, 3, 2):
            sum_two(d, n).wait_recv()
            image_total += ir2[d - 1, :, half[n]].astype(F32)
        image_total = image_total.astype(BF16)
        spread = jnp.concatenate([tn_dot(image_map[b], image_total) for b in range(2)], axis=1)
        spots[:, :, chunk[n]] = spread.astype(BF16).reshape(8, 16, CHUNK)

        @pl.when(odd)
        def _():
            spot_swap(n).start()

    def image_end(n):
        @pl.when(even)
        def _():
            out_ref[:, chunk[n]] = (state[:, chunk[n]] + spots[z, :, chunk[n]].astype(F32)).astype(BF16)

        @pl.when(odd)
        def _():
            spot_swap(n).wait_recv()
            out_ref[:, chunk[n]] = (state[:, chunk[n]] + spot_recv[:, chunk[n]].astype(F32)).astype(BF16)

    text_down(0)
    text_down(1)
    image_step(3)
    text_down(2)
    text_down(3)
    combine(0)
    combine(1)
    image_ready()
    image_down(0)
    image_down(1)
    image_down(2)
    image_down(3)
    combine(2)
    finish(0)
    image_turn(0)
    image_turn(1)
    combine(3)
    finish(1)
    image_turn(2)
    image_turn(3)
    image_out(0)
    finish(2)
    image_out(1)
    image_end(0)
    image_out(2)
    image_end(1)
    image_out(3)
    image_end(2)
    finish(3)
    image_end(3)

    meta_copy.wait_send()
    for copy in kv[0] + kv[1] + swap + swaps + sums:
        copy.wait_send()
    for h in range(2):
        def sent_a(j):
            q_copy(h, j).wait_send()
            back(h, j).wait_send()

        each(1, 8, sent_a)
    for dz in range(-3, 5):
        image_pass(dz).wait_send()
    for i in range(4):
        for side in range(2):
            image_ring(side, i, i).wait_send()
    for n in range(CHUNKS):
        def sent_b(t):
            text_copy(t, n).wait_send()
            text_back(t, n).wait_send()

        each(1, 16, sent_b)
        for d in (1, 2, 3):
            first_hop(d, n).wait_send()
            second_hop(d, n).wait_send()
            sum_one(d, n).wait_send()
            sum_two(d, n).wait_send()
            for core in range(2):
                to_owner(d, core, n).wait_send()

        for side, i in ((0, 0), (1, 0), (0, 1)):
            ring_copy(side, i, n).wait_send()

        @pl.when(odd)
        def _():
            pair_copy(n).wait_send()
            spot_swap(n).wait_send()
            for core in range(2):
                to_owner(0, core, n).wait_send()

        @pl.when(even)
        def _():
            ring_copy(1, 1, n).wait_send()
            to_owner(0, 1 - k, n).wait_send()


def body(
    query, keys, values, resid, flags, routes, gates, out_weight, norm_gain,
    img_gate, img_up, img_down, exp_gate, exp_up, exp_down,
):
    vmem, hbm = pl.BlockSpec(memory_space=pltpu.VMEM), pl.BlockSpec(memory_space=pl.ANY)
    dma = pltpu.SemaphoreType.DMA

    def buf(*shape, dtype=BF16):
        return pltpu.VMEM(shape, dtype)

    def pair(*shape):
        return [dma(shape), dma(shape)]

    return pl.pallas_call(
        layer_kernel,
        name="layer",
        out_shape=jax.ShapeDtypeStruct((16, WIDTH), BF16),
        in_specs=[hbm] * 4 + [vmem] * 3 + [hbm, vmem] + [vmem] * 3 + [hbm] * 3,
        out_specs=vmem,
        scratch_shapes=[
            buf(2, 4, 128, 128), buf(2, 4, 128, 128), buf(2, 8, 128, 128), buf(2, 8, 144, 128), buf(2, 8, 144, 128),
            buf(256, WIDTH), buf(16, WIDTH), buf(256, 128),
            buf(2, 4, 16, WIDTH), buf(4, 16, WIDTH), buf(4, 16, WIDTH), buf(3, 16, WIDTH),
            buf(16, WIDTH, dtype=F32), buf(16, WIDE),
            buf(704, WIDTH), buf(704, WIDTH), buf(704, WIDTH), buf(2, 8, 3, 176, 512),
            buf(16, 128, dtype=F32), buf(16, 128, dtype=F32), buf(256, 128), buf(256, 128), buf(2, 16, 128),
            buf(4, 2, 16, WIDE), buf(16, 16, WIDE), buf(16, 16, WIDE), buf(4, 4, 16, PACKED + 128),
            buf(2, 256, 704, dtype=F32),
            buf(16, 16, WIDTH), buf(16, 16, WIDTH), buf(4, 4, 16, PACKED), buf(3, 4, 16, PACKED),
            buf(4, 16, PACKED), buf(3, 16, PACKED), buf(8, 16, WIDTH), buf(8, 16, WIDTH), buf(16, WIDTH, dtype=F32), buf(8, 16, WIDTH), buf(16, WIDTH),
            *pair(2, 2, 4), *pair(2, 8), *pair(2, 8), *pair(CHUNKS), *pair(CHUNKS, 4), dma((11,)),
            *pair(3), dma, dma, *pair(CHUNKS), *pair(2, 2, CHUNKS), *pair(16, CHUNKS),
            *pair(4, CHUNKS), *pair(4, CHUNKS), *pair(2, 4), *pair(8), *pair(16, CHUNKS),
            *pair(4, CHUNKS), *pair(4, CHUNKS), dma((4, 2, CHUNKS)), dma((8, CHUNKS)), *pair(CHUNKS),
        ],
        compiler_params=pltpu.CompilerParams(
            collective_id=1, has_side_effects=True, vmem_limit_bytes=60 << 20
        ),
    )(
        query, keys, values, resid, flags.reshape(1, -1), routes.T, gates.T, out_weight, norm_gain.reshape(1, WIDTH),
        img_gate.T, img_up.T, img_down.T,
        exp_gate.transpose(0, 2, 1), exp_up.transpose(0, 2, 1), exp_down,
    )


def solution(mesh):
    return jax.shard_map(
        body,
        mesh=mesh,
        in_specs=(
            P("ctx", "exp"),
            P("ctx", "exp"),
            P("ctx", "exp"),
            P("ctx", None),
            P("ctx"),
            P("ctx", None),
            P("ctx", None),
            P("exp", None),
            P(),
            P("exp", "ctx"),
            P("exp", "ctx"),
            P("exp", "ctx"),
            P(("ctx", "exp"), None, None),
            P(("ctx", "exp"), None, None),
            P(("ctx", "exp"), None, None),
        ),
        out_specs=P(("ctx", "exp"), None),
        check_vma=False,
    )
```
